32 devices in a mesh: groups: 2 (over y), req: 4 (over x, core), head: 4 (over z).
Axes of the slice: x: 2, y: 2, z: 4, core: 2. Of those that a mesh axis runs over, the one named last changes fastest.
Arguments:
- ssm_state: float32 [64, 128, 64, 128], P(('groups', 'req'), 'head'), parts along dimension 0, may hold values from -6 to 6
- conv_state: float32 [64, 3, 8, 1280], P(('groups', 'req'), None, 'head'), parts along dimension 0, may hold values from -6 to 6
- counts: int32 [8], P('groups'), parts along dimension 0, may hold values from 4 to 8, as said below
- request_slot: int32 [64], P('groups'), parts along dimension 0, may hold values from 0 to 31, as said below
- token_xbc: bfloat16 [2, 64, 8, 1280], P(None, ('groups', 'req'), 'head'), parts along dimension 1, may hold values from -6 to 6
- token_z: bfloat16 [2, 64, 8192], P(None, ('groups', 'req'), 'head'), parts along dimension 1, may hold values from -6 to 6
- token_dt: bfloat16 [2, 64, 128], P(None, ('groups', 'req'), 'head'), parts along dimension 1, may hold values from -6 to 6
- conv_weight: bfloat16 [4, 8, 1280], P(None, 'head'), may hold values from -3 to 3
- conv_bias: bfloat16 [8, 1280], P('head'), may hold values from -2 to 2
- a_log: bfloat16 [128], P('head'), may hold values from 0 to 2.5
- dt_bias: bfloat16 [128], P('head'), may hold values from -4 to -1
- d_skip: bfloat16 [128], P('head'), may hold values from 0.5 to 2
- norm_gain: bfloat16 [8192], P('head'), may hold values from 0.5 to 1.5
- out_weight: bfloat16 [8192, 8192], P('head', 'req'), may hold values from -0.0625 to 0.0625
Outputs:
- layer_out: bfloat16 [2, 64, 8192], P(None, ('groups', 'head'), 'req'), parts along dimension 1
- decode_ssm: float32 [8, 4, 4, 64, 64, 128], P(('groups', 'req'), 'head'), parts along dimension 0
- decode_conv: float32 [8, 4, 4, 3, 4, 1280], P(('groups', 'req'), 'head'), parts along dimension 0
The draws below stay inside these ranges and needn't reach their ends.
There are 2 independent parts, one for each index of `groups`. The reference program is written for one: setup_inputs(seed, part) draws one part's arguments, and reference() takes and returns one part's arrays. A program takes and returns all parts, laid end to end along the dimension named above; an argument that names none is the same for every part. Nothing has to cross between parts.
Inputs may be any that keep to these rules, and one draw needn't show every extreme that they name: `counts`: some prefill group has all 8 rows live, and another has only 4. Slot s lies with index s // 8 of req. request_slot is one-to-one over all rows. The rows of one prefill group name at most 2 slots of any one index of req, and exactly 2 for some.
All inputs are finite; a program needn't handle non-finite values.
Results may differ from the reference program's by a relative error of at most 0.0049.
Values may be sent and summed in bfloat16 or wider, within the bound.
No kernel may reach another device: no remote copies, remote signals or barrier semaphores. Data moves between devices by JAX's collectives and lax.ppermute only.
A program may use at most 192 MiB of HBM per device.

```python
import jax
import jax.numpy as jnp
from jax import lax

H = 128
P_SIZE = 64
N = 128
G = 8
D = 8192
CW = 4
R_PF = 8
STEPS = 2
CPG = 1280
HPD = 32
GPD = 2
SLOT_DEV = 4
REQUESTS = 32
SLOTS = 32
N_REQ = 4
N_HEAD = 4


def routing_plan(key):
    key_offsets, key_order, key_counts, key_full, key_least = jax.random.split(key, 5)
    offsets = jax.random.permutation(key_offsets, N_REQ)
    order_keys = jax.random.split(key_order, N_REQ)
    within = jax.vmap(lambda one_key: jax.random.permutation(one_key, R_PF))(order_keys)
    group_ids = jnp.arange(N_REQ, dtype=jnp.int32)[:, None]
    row_ids = jnp.arange(R_PF, dtype=jnp.int32)[None, :]
    target_row = (group_ids + offsets[row_ids % N_REQ]) % N_REQ
    slot_ids = target_row * R_PF + within[target_row, row_ids]
    live_counts = jax.random.randint(key_counts, (N_REQ,), R_PF // 2, R_PF + 1)
    full_group = jax.random.randint(key_full, (), 0, N_REQ)
    least_group = (full_group + 1 + jax.random.randint(key_least, (), 0, N_REQ - 1)) % N_REQ
    group_list = jnp.arange(N_REQ)
    live_counts = jnp.where(group_list == full_group, R_PF, live_counts)
    live_counts = jnp.where(group_list == least_group, R_PF // 2, live_counts)
    return (slot_ids.reshape(-1).astype(jnp.int32), live_counts.astype(jnp.int32))


def draw_counts(key, part):
    return routing_plan(key)[1]


def draw_request_slot(key, part):
    return routing_plan(key)[0]


def shard_levels(stream_key, shape, shards, least, top_value):
    loudness = 1.0
    for position, shards_of in shards:
        steps = jax.random.uniform(jax.random.fold_in(jax.random.fold_in(stream_key, 6), position), (shards_of,), jnp.float32, least / len(shards), top_value / len(shards))
        loudness = loudness * jnp.repeat(jnp.exp(steps), shape[position] // shards_of).reshape((-1,) + (1,) * (len(shape) - 1 - position))
    return loudness


def gaussian(rng, extent, scale, limit, shards=(), kind=jnp.bfloat16):
    drawn = scale * jax.random.normal(rng, extent, jnp.float32)
    if shards:
        drawn = drawn * shard_levels(rng, extent, shards, -0.22, 0.18)
    return jnp.clip(drawn, -limit, limit).astype(kind)


def setup_inputs(seed: int = 0, part: int = 0) -> dict:
    key_list = jax.random.split(jax.random.key(seed), 15)
    part_keys = jax.random.split(jax.random.fold_in(key_list[14], part), 15)
    ssm_state = gaussian(part_keys[0], (REQUESTS, H, P_SIZE, N), 1.0, 6.0, ((0, 4), (1, 4)), jnp.float32)
    conv_state = gaussian(part_keys[1], (REQUESTS, CW - 1, G, CPG), 1.0, 6.0, ((0, 4), (2, 4)), jnp.float32)
    counts = draw_counts(jax.random.fold_in(jax.random.fold_in(key_list[14], part), 71), part)
    request_slot = draw_request_slot(jax.random.fold_in(jax.random.fold_in(key_list[14], part), 71), part)
    token_xbc = gaussian(part_keys[4], (STEPS, SLOTS, G, CPG), 1.0, 6.0, ((1, 4), (2, 4)))
    token_z = gaussian(part_keys[5], (STEPS, SLOTS, H * P_SIZE), 1.0, 6.0, ((1, 4), (2, 4)))
    token_dt = gaussian(part_keys[6], (STEPS, SLOTS, H), 1.0, 6.0, ((1, 4), (2, 4)))
    conv_weight = gaussian(key_list[7], (CW, G, CPG), 0.5, 3.0, ((1, 4),))
    conv_bias = gaussian(key_list[8], (G, CPG), 0.3, 2.0, ((0, 4),))
    a_log = jnp.clip(2.5 * jax.random.uniform(key_list[9], (H,), jnp.float32) ** shard_levels(key_list[9], (H,), ((0, 4),), -0.2, 0.2), 0.0, 2.5).astype(jnp.bfloat16)
    dt_bias = jnp.clip(-4.0 + 3.0 * jax.random.uniform(key_list[10], (H,), jnp.float32) ** shard_levels(key_list[10], (H,), ((0, 4),), -0.2, 0.2), -4.0, -1.0).astype(jnp.bfloat16)
    d_skip = jnp.clip(0.5 + 1.5 * jax.random.uniform(key_list[11], (H,), jnp.float32) ** shard_levels(key_list[11], (H,), ((0, 4),), -0.2, 0.2), 0.5, 2.0).astype(jnp.bfloat16)
    norm_gain = jnp.clip(1.0 + 0.1 * jax.random.normal(key_list[12], (H * P_SIZE,), jnp.float32), 0.5, 1.5).astype(jnp.bfloat16)
    out_weight = gaussian(key_list[13], (H * P_SIZE, D), (H * P_SIZE) ** -0.5, 0.0625, ((0, 4), (1, 4)))
    return dict(ssm_state=ssm_state, conv_state=conv_state, counts=counts, request_slot=request_slot, token_xbc=token_xbc, token_z=token_z, token_dt=token_dt, conv_weight=conv_weight, conv_bias=conv_bias, a_log=a_log, dt_bias=dt_bias, d_skip=d_skip, norm_gain=norm_gain, out_weight=out_weight)


def advance(ssm_now, conv_now, xbc_now, z_now, dt_now, conv_weight, conv_bias, a_log, dt_bias, d_skip, norm_gain):
    batch = ssm_now.shape[0]
    window = jnp.concatenate([conv_now, xbc_now.astype(jnp.float32)[:, None]], axis=1)
    conv_out = lax.optimization_barrier(jnp.sum(window * conv_weight.astype(jnp.float32)[None], axis=1)) + conv_bias.astype(jnp.float32)[None]
    activated = jax.nn.silu(conv_out)
    groups = activated.shape[1]
    per_group = H // G
    x_width = per_group * P_SIZE
    x_heads = activated[..., :x_width].reshape(batch, groups * per_group, P_SIZE)
    b_heads = jnp.repeat(activated[..., x_width:x_width + N], per_group, axis=1)
    c_heads = jnp.repeat(activated[..., x_width + N:], per_group, axis=1)
    step_size = jax.nn.softplus(dt_now.astype(jnp.float32) + dt_bias.astype(jnp.float32)[None])
    decay_rate = jnp.exp(-step_size * jnp.exp(a_log.astype(jnp.float32))[None])
    ssm_now = decay_rate[..., None, None] * ssm_now + (step_size[..., None] * x_heads)[..., None] * b_heads[:, :, None, :]
    readout = lax.optimization_barrier(jnp.sum(ssm_now * c_heads[:, :, None, :], axis=-1)) + d_skip.astype(jnp.float32)[None, :, None] * x_heads
    gated_y = readout.reshape(batch, -1) * jax.nn.silu(z_now.astype(jnp.float32))
    grouped = gated_y.reshape(batch, groups, x_width)
    normed = grouped * lax.rsqrt(lax.optimization_barrier(jnp.mean(grouped * grouped, axis=-1, keepdims=True)) + 1e-05)
    normed = (normed.reshape(batch, -1) * norm_gain.astype(jnp.float32)[None]).astype(jnp.bfloat16)
    return (ssm_now, window[:, 1:], normed)

def reference(ssm_state, conv_state, counts, request_slot, token_xbc, token_z, token_dt, conv_weight, conv_bias, a_log, dt_bias, d_skip, norm_gain, out_weight):
    row_ids = jnp.arange(REQUESTS, dtype=jnp.int32)
    live_rows = row_ids % R_PF < counts[row_ids // R_PF]
    live_weight = live_rows.astype(jnp.float32)
    start_ssm = jnp.zeros((SLOTS, H, P_SIZE, N), jnp.float32).at[request_slot].set(ssm_state * live_weight[:, None, None, None])
    start_conv = jnp.zeros((SLOTS, CW - 1, G, CPG), jnp.float32).at[request_slot].set(conv_state * live_weight[:, None, None, None])

    def run_slot(items):
        ssm_now, conv_now, xbc_all, z_all, dt_all = items
        ssm_now = ssm_now[None]
        conv_now = conv_now[None]
        outputs = []
        for step_index in range(STEPS):
            ssm_now, conv_now, normed = advance(ssm_now, conv_now, xbc_all[step_index][None], z_all[step_index][None], dt_all[step_index][None], conv_weight, conv_bias, a_log, dt_bias, d_skip, norm_gain)
            outputs.append(normed[0])
        return (ssm_now[0], conv_now[0], jnp.stack(outputs))
    final_ssm, final_conv, normed_all = lax.map(run_slot, (start_ssm, start_conv, jnp.swapaxes(token_xbc, 0, 1), jnp.swapaxes(token_z, 0, 1), jnp.swapaxes(token_dt, 0, 1)))
    layer_out = jnp.stack([jnp.dot(normed_all[:, step_index], out_weight, preferred_element_type=jnp.float32).astype(jnp.bfloat16) for step_index in range(STEPS)])
    half_count = N_HEAD // 2
    decode_ssm = final_ssm.reshape(N_REQ, 2, SLOT_DEV, half_count, 2 * HPD, P_SIZE, N).transpose(0, 3, 1, 2, 4, 5, 6).reshape(N_REQ, N_HEAD, SLOT_DEV, 2 * HPD, P_SIZE, N)
    decode_conv = final_conv.reshape(N_REQ, 2, SLOT_DEV, CW - 1, half_count, 2 * GPD, CPG).transpose(0, 4, 1, 2, 3, 5, 6).reshape(N_REQ, N_HEAD, SLOT_DEV, CW - 1, 2 * GPD, CPG)
    return (layer_out, decode_ssm, decode_conv)
```

```python
import functools

import jax
import jax.numpy as jnp
from jax import lax
from jax.experimental import pallas as pl
from jax.experimental.pallas import tpu as pltpu
from jax.sharding import PartitionSpec as P

H = 128
P_SIZE = 64
N = 128
G = 8
R_PF = 8
PER_GROUP = H // G
X_WIDTH = PER_GROUP * P_SIZE
CHUNKS = 8
AHEAD = 3
VMEM_LIMIT = 48 * 1024 * 1024

ANY = pl.BlockSpec(memory_space=pl.ANY)


def split_bf16(value):
    high = value.astype(jnp.bfloat16)
    low = (value - high.astype(jnp.float32)).astype(jnp.bfloat16)
    return high, low


def pack_kernel(count, cap, _rows, *refs):
    inputs, outputs = refs[:count], refs[-(count // cap) :]
    for place in range(count):
        outputs[place // cap][place % cap] = inputs[place][0].astype(jnp.bfloat16)


def pack_chunk(ssm_state, row_of, chunk, width, cap, after):
    count = row_of.shape[0]
    block = (1, width, P_SIZE, N)
    specs = [
        pl.BlockSpec(block, functools.partial(lambda i, rows, p: (rows[p], chunk, 0, 0), p=p))
        for p in range(count)
    ]
    shape = (cap, width, P_SIZE, N)
    return pl.pallas_call(
        functools.partial(pack_kernel, count, cap),
        grid_spec=pltpu.PrefetchScalarGridSpec(
            num_scalar_prefetch=1,
            grid=(1,),
            in_specs=specs + [ANY] * len(after),
            out_specs=[pl.BlockSpec(shape, lambda i, rows: (0, 0, 0, 0))] * (count // cap),
        ),
        out_shape=[jax.ShapeDtypeStruct(shape, jnp.bfloat16)] * (count // cap),
        compiler_params=pltpu.CompilerParams(vmem_limit_bytes=VMEM_LIMIT),
        cost_estimate=pl.CostEstimate(
            flops=0, bytes_accessed=6 * count * width * P_SIZE * N, transcendentals=0
        ),
        name="pack",
    )(row_of, *([ssm_state] * count), *after)


def route_kernel(sources, cap, places, *refs):
    arrived, keep, give, sems = refs[:sources], refs[-3], refs[-2], refs[-1]
    half = keep.shape[0]

    def copy(index, source):
        target = keep if index < half else give
        rank = places[index] % cap
        return pltpu.make_async_copy(
            arrived[source].at[rank], target.at[index % half], sems.at[index]
        )

    for index in range(2 * half):
        for source in range(sources):

            @pl.when(places[index] // cap == source)
            def _():
                copy(index, source).start()

    for index in range(2 * half):
        copy(index, 0).wait()


def route_chunk(arrived, places, half, after):
    cap = arrived[0].shape[0]
    shape = (half,) + arrived[0].shape[1:]
    out = jax.ShapeDtypeStruct(shape, jnp.bfloat16)
    return pl.pallas_call(
        functools.partial(route_kernel, len(arrived), cap),
        grid_spec=pltpu.PrefetchScalarGridSpec(
            num_scalar_prefetch=1,
            grid=(1,),
            in_specs=[ANY] * (len(arrived) + len(after)),
            out_specs=[ANY, ANY],
            scratch_shapes=[pltpu.SemaphoreType.DMA((2 * half,))],
        ),
        out_shape=[out, out],
        cost_estimate=pl.CostEstimate(
            flops=0, bytes_accessed=8 * half * arrived[0][0].size, transcendentals=0
        ),
        name="route",
    )(places, *arrived, *after)


def readout_kernel(state, taps, out):
    rows = state[0].reshape(X_WIDTH, N)
    state_high, state_low = split_bf16(rows)
    both = jnp.concatenate(split_bf16(taps[0, 0]), axis=0)
    dims = (((1,), (1,)), ((), ()))
    total = lax.dot_general(both, state_high, dims, preferred_element_type=jnp.float32)
    total = total + lax.dot_general(both, state_low, dims, preferred_element_type=jnp.float32)
    out[0, 0] = total[:8] + total[8:]


def readout(ssm_state, taps):
    rows, groups = taps.shape[:2]
    return pl.pallas_call(
        readout_kernel,
        grid=(rows, groups),
        in_specs=[
            pl.BlockSpec((1, PER_GROUP, P_SIZE, N), lambda i, g: (i, g, 0, 0)),
            pl.BlockSpec((1, 1, 8, N), lambda i, g: (i, g, 0, 0)),
        ],
        out_specs=pl.BlockSpec((1, 1, 8, X_WIDTH), lambda i, g: (i, g, 0, 0)),
        out_shape=jax.ShapeDtypeStruct((rows, groups, 8, X_WIDTH), jnp.float32),
        compiler_params=pltpu.CompilerParams(vmem_limit_bytes=VMEM_LIMIT),
        cost_estimate=pl.CostEstimate(
            flops=64 * ssm_state.size, bytes_accessed=4 * ssm_state.size, transcendentals=0
        ),
        name="readout",
    )(ssm_state, taps)


def finish_kernel(width, heads, base, _half, decay, keep, got, update, taps, *refs):
    out = refs[-1]
    owner, slot = pl.program_id(0), pl.program_id(1)
    update_high, update_low = split_bf16(update[0, 0, 0])
    taps_high, taps_low = split_bf16(taps[0, 0, 0])
    added = lax.dot_general(
        jnp.concatenate([update_high, update_low, update_high, update_low], axis=0),
        jnp.concatenate([taps_high, taps_high, taps_low, taps_low], axis=0),
        (((0,), (0,)), ((), ())),
        preferred_element_type=jnp.float32,
    ).reshape(width, P_SIZE, N)
    first = (owner * pl.num_programs(1) + slot) * heads + base

    def fill(source):
        for head in range(width):
            out[0, 0, 0, head] = (
                decay[first + head] * source[0, head].astype(jnp.float32) + added[head]
            )

    pl.when(owner == 0)(lambda: fill(keep))
    pl.when(owner == 1)(lambda: fill(got))


def finish_chunk(so_far, keep, got, half_index, decay, update, taps, chunk, heads):
    slots, width = keep.shape[:2]
    per_half = heads // width
    per_group = X_WIDTH // (width * P_SIZE)
    group, part = chunk // per_group, chunk % per_group
    out_shape = jax.ShapeDtypeStruct((1, 1, slots, 2 * heads, P_SIZE, N), jnp.float32)
    block = (1, width, P_SIZE, N)
    extra = [] if so_far is None else [so_far]
    return pl.pallas_call(
        functools.partial(finish_kernel, width, heads, chunk * width),
        grid_spec=pltpu.PrefetchScalarGridSpec(
            num_scalar_prefetch=2,
            grid=(2, slots),
            in_specs=[
                pl.BlockSpec(block, lambda o, j, h, d: (jnp.where(o == 0, j, slots - 1), 0, 0, 0)),
                pl.BlockSpec(block, lambda o, j, h, d: (jnp.where(o == 0, 0, j), 0, 0, 0)),
                pl.BlockSpec((1, 1, 1, 8, width * P_SIZE), lambda o, j, h, d: (o, j, group, 0, part)),
                pl.BlockSpec((1, 1, 1, 8, N), lambda o, j, h, d: (o, j, group, 0, 0)),
            ]
            + [ANY] * len(extra),
            out_specs=pl.BlockSpec(
                (1, 1, 1, width, P_SIZE, N),
                lambda o, j, h, d: (0, 0, j, h[o] * per_half + chunk, 0, 0),
            ),
        ),
        out_shape=out_shape,
        input_output_aliases={6: 0} if extra else {},
        compiler_params=pltpu.CompilerParams(vmem_limit_bytes=VMEM_LIMIT),
        cost_estimate=pl.CostEstimate(
            flops=64 * slots * width * P_SIZE * N,
            bytes_accessed=12 * slots * width * P_SIZE * N,
            transcendentals=0,
        ),
        name="finish",
    )(half_index, decay, keep, got, update, taps, *extra)


def take_rows(values, index, axis=0):
    return jnp.take(values, index, axis=axis, mode="clip")


def on_device(
    ssm_state,
    conv_state,
    counts,
    request_slot,
    token_xbc,
    token_z,
    token_dt,
    conv_weight,
    conv_bias,
    a_log,
    dt_bias,
    d_skip,
    norm_gain,
    out_weight,
):
    f32 = jnp.float32
    req_count = lax.axis_size("req")
    head_count = lax.axis_size("head")
    my_req = lax.axis_index("req")
    parity = lax.axis_index("head") % 2
    cap = (R_PF + req_count - 1) // req_count
    slot_dev = R_PF // 2
    steps = token_xbc.shape[0]
    heads = ssm_state.shape[1]
    groups = conv_state.shape[2]
    width = heads // CHUNKS
    channels = groups * X_WIDTH
    conv_width = conv_state.shape[3]

    order = jnp.arange(R_PF, dtype=jnp.int32)
    my_slots = lax.dynamic_slice_in_dim(request_slot, my_req * R_PF, R_PF)
    my_dest = my_slots // R_PF
    my_rank = jnp.sum(
        ((my_dest[:, None] == my_dest[None, :]) & (order[None, :] < order[:, None])).astype(jnp.int32),
        axis=1,
    )
    place = jnp.arange(req_count * cap, dtype=jnp.int32)
    row_of = jnp.sum(
        jnp.where(
            ((my_dest ^ my_req) * cap + my_rank)[None, :] == place[:, None], order[None, :], 0
        ),
        axis=1,
    )
    my_live = order < lax.dynamic_index_in_dim(counts, my_req, 0, keepdims=False)

    all_dest = (request_slot // R_PF).reshape(req_count, R_PF)
    all_rank = jnp.sum(
        (
            (all_dest[:, :, None] == all_dest[:, None, :]) & (order[None, None, :] < order[None, :, None])
        ).astype(jnp.int32),
        axis=2,
    )
    row_ids = jnp.arange(req_count * R_PF, dtype=jnp.int32)
    local_slots = my_req * R_PF + order
    names = request_slot[None, :] == local_slots[:, None]
    rank_row = all_rank.reshape(-1)
    slot_place = jnp.sum(
        jnp.where(names, ((row_ids // R_PF) * cap + rank_row)[None, :], 0), axis=1
    )
    slot_shift = jnp.sum(
        jnp.where(names, ((row_ids // R_PF ^ my_req) * cap + rank_row)[None, :], 0), axis=1
    )
    mine = parity * slot_dev + jnp.arange(slot_dev, dtype=jnp.int32)
    theirs = (1 - parity) * slot_dev + jnp.arange(slot_dev, dtype=jnp.int32)
    split = jnp.concatenate([mine, theirs])
    places = slot_shift[split]

    def swap(value):
        return lax.ppermute(value, "head", [(i, i ^ 1) for i in range(head_count)])

    def exchange(value):
        return lax.all_to_all(value, "req", split_axis=0, concat_axis=0, tiled=True)

    keeps, gots = [], []
    for chunk in range(CHUNKS):
        after = [gots[chunk - AHEAD]] if chunk >= AHEAD else []
        packed = pack_chunk(ssm_state, row_of, chunk, width, cap, after)
        arrived = [packed[0]]
        for shift in range(1, req_count):
            pairs = [(i, i ^ shift) for i in range(req_count)]
            arrived.append(lax.ppermute(packed[shift], "req", pairs))
        keep, give = route_chunk(arrived, places, slot_dev, gots[chunk - 1 : chunk])
        keeps.append(keep)
        gots.append(swap(give))

    tokens = jnp.concatenate(
        [
            token_xbc.reshape(steps, R_PF, -1),
            token_z.reshape(steps, R_PF, -1),
            token_dt.reshape(steps, R_PF, -1),
        ],
        axis=2,
    )
    slot_at = jnp.sum(
        jnp.where(slot_place[None, :] == place[:, None], order[None, :], 0), axis=1
    )
    tokens = exchange(jnp.swapaxes(take_rows(tokens, slot_at, 1), 0, 1))
    my_place = my_dest * cap + my_rank
    tokens = take_rows(tokens, my_place)
    xbc_size = groups * conv_width
    row_xbc = tokens[:, :, :xbc_size].reshape(R_PF, steps, groups, conv_width).astype(f32)
    row_z = tokens[:, :, xbc_size : xbc_size + channels].astype(f32)
    row_dt = tokens[:, :, xbc_size + channels :].astype(f32)

    conv_now = jnp.where(my_live[:, None, None, None], conv_state, 0.0)
    window = jnp.concatenate([conv_now, row_xbc], axis=1)
    taps = conv_weight.shape[0]
    weight = conv_weight.astype(f32)
    act = jnp.stack(
        [
            jax.nn.silu(
                sum(window[:, t + k] * weight[k][None] for k in range(taps))
                + conv_bias.astype(f32)[None]
            )
            for t in range(steps)
        ],
        axis=1,
    )
    x = act[..., :X_WIDTH]
    b = act[..., X_WIDTH : X_WIDTH + N]
    c = act[..., X_WIDTH + N :]
    dt = jax.nn.softplus(row_dt + dt_bias.astype(f32))
    decay = jnp.exp(-dt * jnp.exp(a_log.astype(f32)))

    def spread(value):
        shape = value.shape[:-1] + (groups, PER_GROUP, P_SIZE)
        value = value.reshape(value.shape[:-1] + (groups, PER_GROUP, 1))
        return jnp.broadcast_to(value, shape).reshape(shape[:-2] + (X_WIDTH,))

    u = spread(dt) * x
    wide_decay = spread(decay)
    pad = jnp.zeros((R_PF, groups, 8 - steps, N), f32)
    read = readout(ssm_state, jnp.concatenate([jnp.swapaxes(c, 1, 2), pad], axis=2))
    read = jnp.where(my_live[:, None, None, None], read, 0.0)
    skip = spread(d_skip.astype(f32))

    def pair_sum(first, second):
        return jnp.sum(first * second, axis=-1, keepdims=True)

    y0 = wide_decay[:, 0] * read[:, :, 0] + pair_sum(b[:, 0], c[:, 0]) * u[:, 0] + skip * x[:, 0]
    y1 = (
        wide_decay[:, 1]
        * (wide_decay[:, 0] * read[:, :, 1] + pair_sum(b[:, 0], c[:, 1]) * u[:, 0])
        + pair_sum(b[:, 1], c[:, 1]) * u[:, 1]
        + skip * x[:, 1]
    )
    gated = jnp.stack([y0, y1]) * jax.nn.silu(
        jnp.swapaxes(row_z, 0, 1).reshape(steps, R_PF, groups, X_WIDTH)
    )
    normed = gated * lax.rsqrt(jnp.mean(gated * gated, axis=-1, keepdims=True) + 1e-05)
    normed = (normed.reshape(steps, R_PF, channels) * norm_gain.astype(f32)).astype(jnp.bfloat16)

    slot_row = jnp.sum(
        jnp.where(request_slot[None, :] == row_ids[:, None], row_ids[None, :], 0), axis=1
    )
    normed_all = take_rows(lax.all_gather(normed, "req", axis=1, tiled=True), slot_row, 1)
    projected = jnp.einsum("tsc,cd->tsd", normed_all, out_weight, preferred_element_type=f32)
    layer_out = lax.psum_scatter(projected, "head", scatter_dimension=1, tiled=True).astype(
        jnp.bfloat16
    )

    packet = jnp.concatenate(
        [
            (wide_decay[:, 1] * u[:, 0]).reshape(R_PF, -1),
            u[:, 1].reshape(R_PF, -1),
            b[:, 0].reshape(R_PF, -1),
            b[:, 1].reshape(R_PF, -1),
            window[:, 2].reshape(R_PF, -1),
            jnp.where(my_live[:, None], decay[:, 0] * decay[:, 1], 0.0),
        ],
        axis=1,
    )
    row_at = jnp.sum(jnp.where(my_place[None, :] == place[:, None], order[None, :], 0), axis=1)
    packet = exchange(take_rows(packet, row_at))
    local_tokens = jnp.swapaxes(token_xbc, 0, 1).reshape(R_PF, -1).astype(f32)
    by_slot = jnp.concatenate([take_rows(packet, slot_place), local_tokens], axis=1)
    by_slot = take_rows(by_slot, split)
    own, other = by_slot[:slot_dev], swap(by_slot[slot_dev:])
    both = jnp.stack([own, other])

    def cut(start, size):
        return both[:, :, start : start + size]

    at = 0
    u0, at = cut(at, channels), at + channels
    u1, at = cut(at, channels), at + channels
    b0, at = cut(at, groups * N), at + groups * N
    b1, at = cut(at, groups * N), at + groups * N
    last, at = cut(at, xbc_size), at + xbc_size
    total_decay, at = cut(at, heads), at + heads
    fresh = cut(at, steps * xbc_size)

    def pile(first, second, size):
        shape = (2, slot_dev, groups, 1, size)
        zero = jnp.zeros((2, slot_dev, groups, 8 - steps, size), f32)
        return jnp.concatenate([first.reshape(shape), second.reshape(shape), zero], axis=3)

    update = pile(u0, u1, X_WIDTH)
    update_taps = pile(b0, b1, N)
    half_index = jnp.stack([parity, 1 - parity])
    flat_decay = total_decay.reshape(-1)
    out_ssm = None
    for chunk in range(CHUNKS):
        out_ssm = finish_chunk(
            out_ssm, keeps[chunk], gots[chunk], half_index, flat_decay, update, update_taps, chunk, heads
        )

    conv_rows = jnp.concatenate([last, fresh], axis=2).reshape(
        2, slot_dev, 1 + steps, groups, conv_width
    )
    conv_rows = jnp.where(parity == 0, conv_rows, conv_rows[::-1])
    out_conv = jnp.moveaxis(conv_rows, 0, 2).reshape(
        1, 1, slot_dev, 1 + steps, 2 * groups, conv_width
    )
    return (layer_out, out_ssm, out_conv)


def solution(mesh):
    in_specs = (
        P(("groups", "req"), "head", None, None),
        P(("groups", "req"), None, "head", None),
        P("groups"),
        P("groups"),
        P(None, ("groups", "req"), "head", None),
        P(None, ("groups", "req"), "head"),
        P(None, ("groups", "req"), "head"),
        P(None, "head", None),
        P("head", None),
        P("head"),
        P("head"),
        P("head"),
        P("head"),
        P("head", "req"),
    )
    out_specs = (
        P(None, ("groups", "head"), "req"),
        P(("groups", "req"), "head", None, None, None, None),
        P(("groups", "req"), "head", None, None, None, None),
    )
    return jax.shard_map(
        on_device, mesh=mesh, in_specs=in_specs, out_specs=out_specs, check_vma=False
    )
```

```python
import functools

import jax
import jax.numpy as jnp
from jax import lax
from jax.experimental import pallas as pl
from jax.experimental.pallas import tpu as pltpu
from jax.sharding import PartitionSpec as P

H = 128
P_SIZE = 64
N = 128
G = 8
R_PF = 8
PER_GROUP = H // G
X_WIDTH = PER_GROUP * P_SIZE
CHUNKS = 4
AHEAD = 2
LANES = 128
VMEM_LIMIT = 48 * 1024 * 1024

ANY = pl.BlockSpec(memory_space=pl.ANY)


def split_bf16(value):
    high = value.astype(jnp.bfloat16)
    low = (value - high.astype(jnp.float32)).astype(jnp.bfloat16)
    return high, low


class Plan:
    def __init__(self, req_count):
        self.cap = (R_PF + req_count - 1) // req_count
        self.places = req_count * self.cap
        self.rows = req_count * R_PF
        self.row_of = 0
        self.row_place = self.row_of + self.places
        self.slot_place = self.row_place + R_PF
        self.split_place = self.slot_place + R_PF
        self.live = self.split_place + R_PF
        self.parity = self.live + 1
        self.slot_row = self.parity + 1
        self.size = self.slot_row + self.rows


def plan_kernel(plan, request_slot, counts, out):
    me = lax.axis_index("req")
    parity = lax.axis_index("head") % 2
    half = R_PF // 2
    out[plan.live] = counts[me]
    out[plan.parity] = parity
    for place in range(plan.places):
        out[plan.row_of + place] = 0

    dests = [request_slot[me * R_PF + row] // R_PF for row in range(R_PF)]
    for row in range(R_PF):
        rank = sum([(dests[row] == dests[other]).astype(jnp.int32) for other in range(row)], 0)
        out[plan.row_place + row] = dests[row] * plan.cap + rank
        out[plan.row_of + (dests[row] ^ me) * plan.cap + rank] = row

    @pl.loop(0, plan.rows // R_PF)
    def _(group):
        seen = jnp.int32(0)
        for row in range(R_PF):
            slot = request_slot[group * R_PF + row]
            out[plan.slot_row + slot] = group * R_PF + row
            here = slot // R_PF == me
            local = slot % R_PF

            @pl.when(here)
            def _():
                out[plan.slot_place + local] = group * plan.cap + seen
                out[plan.split_place + (local + parity * half) % R_PF] = (
                    group ^ me
                ) * plan.cap + seen

            seen = seen + here.astype(jnp.int32)


def make_plan(plan, request_slot, counts):
    smem = pl.BlockSpec(memory_space=pltpu.SMEM)
    return pl.pallas_call(
        functools.partial(plan_kernel, plan),
        in_specs=[smem, smem],
        out_specs=smem,
        out_shape=jax.ShapeDtypeStruct((plan.size,), jnp.int32),
        name="plan",
    )(request_slot, counts)


def one_hot(shape, pairs):
    rows = lax.broadcasted_iota(jnp.int32, shape, 0)
    columns = lax.broadcasted_iota(jnp.int32, shape, 1)
    total = jnp.zeros(shape, jnp.float32)
    for row, column in pairs:
        total = jnp.where((rows == row) & (columns == column), 1.0, total)
    return total.astype(jnp.bfloat16)


def pick(matrix, values):
    return jnp.dot(matrix, values, preferred_element_type=jnp.float32)


def tokens_kernel(plan, table, xbc, z, dt, out):
    steps, groups = xbc.shape[:2]
    matrix = one_hot(
        (plan.places, R_PF), [(table[plan.slot_place + slot], slot) for slot in range(R_PF)]
    )

    def put(values, start):
        picked = pick(matrix, values)
        size = values.shape[1]
        for source in range(plan.places // plan.cap):
            rows = picked[source * plan.cap : (source + 1) * plan.cap]
            out[source, :, start : start + size] = rows.astype(jnp.bfloat16)

    at = 0
    for step in range(steps):
        for group in range(groups):
            put(xbc[step, group], at)
            at += xbc.shape[3]
        put(z[step], at)
        at += z.shape[2]
        put(dt[step], at)
        at += LANES


def pack_tokens(plan, table, xbc, z, dt):
    steps, groups = xbc.shape[:2]
    size = steps * (groups * xbc.shape[3] + z.shape[2] + LANES)
    return pl.pallas_call(
        functools.partial(tokens_kernel, plan),
        grid_spec=pltpu.PrefetchScalarGridSpec(
            num_scalar_prefetch=1,
            grid=(1,),
            in_specs=[whole(xbc), whole(z), whole(dt)],
            out_specs=pl.BlockSpec((plan.places // plan.cap, plan.cap, size), lambda i, t: (0, 0, 0)),
        ),
        out_shape=jax.ShapeDtypeStruct((plan.places // plan.cap, plan.cap, size), jnp.bfloat16),
        name="tokens",
    )(table, xbc, z, dt)


def whole(array):
    return pl.BlockSpec(array.shape, lambda *_: (0,) * array.ndim)


def silu(value):
    return value / (1.0 + jnp.exp(-value))


def rows_kernel(plan, table, tokens, conv, weight, bias, small, gain, state, *refs):
    normed, packet, read, read_taps, acts, wide, gates, lines = refs
    steps = 2
    taps, groups, conv_width = weight.shape
    heads = state.shape[1]
    channels = groups * X_WIDTH
    index = pl.program_id(0)
    row_ids = lax.broadcasted_iota(jnp.int32, (R_PF, 1), 0)
    live = row_ids < table[plan.live]
    f32, bf16 = jnp.float32, jnp.bfloat16
    update_at = 0
    taps_at = update_at + steps * channels
    last_at = taps_at + steps * groups * N
    decay_at = last_at + groups * conv_width

    @pl.when(index == 0)
    def _():
        matrix = one_hot(
            (R_PF, plan.places), [(row, table[plan.row_place + row]) for row in range(R_PF)]
        )
        stride = tokens.shape[2] // steps

        def rows_of(start, size):
            parts = [tokens[source, :, start : start + size] for source in range(tokens.shape[0])]
            parts = jnp.concatenate([part.astype(f32) for part in parts], axis=0)
            return pick(matrix, parts.astype(bf16))

        for group in range(groups):
            window = [
                jnp.where(live, conv[tap, group], 0.0) for tap in range(taps - 1)
            ] + [
                rows_of(step * stride + group * conv_width, conv_width) for step in range(steps)
            ]
            kernel = [weight[tap].astype(f32)[group : group + 1] for tap in range(taps)]
            offset = bias[...].astype(f32)[group : group + 1]
            parts = []
            for step in range(steps):
                total = sum(window[step + tap] * kernel[tap] for tap in range(taps)) + offset
                act = silu(total)
                acts[step, group] = act
                parts.append(act[:, X_WIDTH + N :])
            high = [part.astype(bf16).astype(f32) for part in parts]
            low = [part - near for part, near in zip(parts, high)]
            read_taps[group] = jnp.concatenate(high + low, axis=0).astype(bf16)
            start = last_at + group * conv_width
            lines[:, start : start + conv_width] = window[taps - 2]

        dts, decays = [], []
        rate = jnp.exp(small[0:1, :heads])
        for step in range(steps):
            base = step * stride + groups * conv_width
            gates[step] = silu(rows_of(base, channels))
            raw = rows_of(base + channels, LANES)[:, :heads] + small[1:2, :heads]
            dts.append(jnp.maximum(raw, 0.0) + jnp.log1p(jnp.exp(-jnp.abs(raw))))
            decays.append(jnp.exp(-dts[-1] * rate))
        lines[:, decay_at : decay_at + LANES] = jnp.concatenate(
            [jnp.where(live, decays[0] * decays[1], 0.0), jnp.zeros((R_PF, LANES - heads), f32)],
            axis=1,
        )
        skip = jnp.broadcast_to(small[2:3, :heads], (R_PF, heads))
        narrow = jnp.concatenate(dts + decays + [skip], axis=0)
        high = narrow.astype(bf16).astype(f32)
        middle = (narrow - high).astype(bf16).astype(f32)
        narrow = jnp.concatenate([high, middle, narrow - high - middle], axis=1).astype(bf16)
        head_ids = lax.broadcasted_iota(jnp.int32, (3 * heads, channels), 0) % heads
        channel_ids = lax.broadcasted_iota(jnp.int32, (3 * heads, channels), 1) // P_SIZE
        spread = pick(narrow, (head_ids == channel_ids).astype(bf16))
        for part in range(5):
            wide[part] = spread[part * R_PF : (part + 1) * R_PF]

    for group in range(groups):
        rows = state[0, group * PER_GROUP : (group + 1) * PER_GROUP].reshape(X_WIDTH, N)
        state_high, state_low = split_bf16(rows)
        dims = (((1,), (1,)), ((), ()))
        total = lax.dot_general(read_taps[group], state_high, dims, preferred_element_type=f32)
        rest = lax.dot_general(
            read_taps[group, : steps * R_PF], state_low, dims, preferred_element_type=f32
        )
        total = total[: steps * R_PF] + total[steps * R_PF :] + rest
        for step in range(steps):
            part = total[step * R_PF : (step + 1) * R_PF]
            read[group, step] = jnp.where(row_ids == index, part, read[group, step])

    @pl.when(index == R_PF - 1)
    def _():
        for group in range(groups):
            span = slice(group * X_WIDTH, (group + 1) * X_WIDTH)
            x = [acts[step, group, :, :X_WIDTH] for step in range(steps)]
            b = [acts[step, group, :, X_WIDTH : X_WIDTH + N] for step in range(steps)]
            c = [acts[step, group, :, X_WIDTH + N :] for step in range(steps)]
            u = [wide[step, :, span] * x[step] for step in range(steps)]
            first_decay, second_decay, skip = wide[2, :, span], wide[3, :, span], wide[4, :, span]
            held = [jnp.where(live, read[group, step], 0.0) for step in range(steps)]

            def pair_sum(one, two):
                return jnp.sum(one * two, axis=1, keepdims=True)

            later = second_decay * u[0]
            y = [
                first_decay * held[0] + pair_sum(b[0], c[0]) * u[0] + skip * x[0],
                second_decay * first_decay * held[1]
                + pair_sum(b[0], c[1]) * later
                + pair_sum(b[1], c[1]) * u[1]
                + skip * x[1],
            ]
            result = []
            for step in range(steps):
                gated = y[step] * gates[step, :, span]
                scale = lax.rsqrt(jnp.mean(gated * gated, axis=1, keepdims=True) + 1e-05)
                result.append(gated * scale * gain[0:1, span])
            normed[:, span] = jnp.concatenate(result, axis=0).astype(bf16)
            lines[:, span] = later
            lines[:, channels + group * X_WIDTH : channels + (group + 1) * X_WIDTH] = u[1]
            for step in range(steps):
                start = taps_at + (step * groups + group) * N
                lines[:, start : start + N] = b[step]
        for row in range(R_PF):
            packet[table[plan.row_place + row]] = lines[row : row + 1]


def run_rows(plan, table, tokens, conv, weight, bias, small, gain, ssm_state):
    taps, groups, conv_width = weight.shape
    steps = 2
    heads = ssm_state.shape[1]
    channels = groups * X_WIDTH
    size = steps * channels + steps * groups * N + groups * conv_width + LANES
    f32 = jnp.float32
    return pl.pallas_call(
        functools.partial(rows_kernel, plan),
        grid_spec=pltpu.PrefetchScalarGridSpec(
            num_scalar_prefetch=1,
            grid=(R_PF,),
            in_specs=[
                whole(tokens),
                whole(conv),
                whole(weight),
                whole(bias),
                whole(small),
                whole(gain),
                pl.BlockSpec((1, heads, P_SIZE, N), lambda i, t: (i, 0, 0, 0)),
            ],
            out_specs=[
                pl.BlockSpec((steps * R_PF, channels), lambda i, t: (0, 0)),
                pl.BlockSpec((plan.places, 1, size), lambda i, t: (0, 0, 0)),
            ],
            scratch_shapes=[
                pltpu.VMEM((groups, steps, R_PF, X_WIDTH), f32),
                pltpu.VMEM((groups, 2 * steps * R_PF, N), jnp.bfloat16),
                pltpu.VMEM((steps, groups, R_PF, conv_width), f32),
                pltpu.VMEM((5, R_PF, channels), f32),
                pltpu.VMEM((steps, R_PF, channels), f32),
                pltpu.VMEM((R_PF, size), f32),
            ],
        ),
        out_shape=[
            jax.ShapeDtypeStruct((steps * R_PF, channels), jnp.bfloat16),
            jax.ShapeDtypeStruct((plan.places, 1, size), f32),
        ],
        compiler_params=pltpu.CompilerParams(vmem_limit_bytes=VMEM_LIMIT),
        cost_estimate=pl.CostEstimate(
            flops=64 * ssm_state.size, bytes_accessed=4 * ssm_state.size, transcendentals=0
        ),
        name="rows",
    )(table, tokens, conv, weight, bias, small, gain, ssm_state)


def project_kernel(plan, share, table, normed, weight, out, picked):
    steps = 2

    @pl.when(pl.program_id(0) == 0)
    def _():
        shape = (steps * plan.rows, steps * plan.rows)
        rows = lax.broadcasted_iota(jnp.int32, shape, 0)
        columns = lax.broadcasted_iota(jnp.int32, shape, 1)

        def add(slot, total):
            row = table[plan.slot_row + slot]
            target = (slot // share) * steps * share + slot % share
            source = (row // R_PF) * steps * R_PF + row % R_PF
            for step in range(steps):
                hit = (rows == target + step * share) & (columns == source + step * R_PF)
                total = jnp.where(hit, 1.0, total)
            return total

        matrix = lax.fori_loop(0, plan.rows, add, jnp.zeros(shape, jnp.float32), unroll=8)
        picked[...] = pick(matrix.astype(jnp.bfloat16), normed[...]).astype(jnp.bfloat16)

    out[...] = pick(picked[...], weight[...])


def project(plan, share, table, normed, weight):
    rows, depth = normed.shape
    columns = weight.shape[1]
    block = min(512, columns)
    return pl.pallas_call(
        functools.partial(project_kernel, plan, share),
        grid_spec=pltpu.PrefetchScalarGridSpec(
            num_scalar_prefetch=1,
            grid=(columns // block,),
            in_specs=[whole(normed), pl.BlockSpec((depth, block), lambda i, t: (0, i))],
            out_specs=pl.BlockSpec((rows, block), lambda i, t: (0, i)),
            scratch_shapes=[pltpu.VMEM((rows, depth), jnp.bfloat16)],
        ),
        out_shape=jax.ShapeDtypeStruct((rows, columns), jnp.float32),
        compiler_params=pltpu.CompilerParams(vmem_limit_bytes=VMEM_LIMIT),
        cost_estimate=pl.CostEstimate(
            flops=2 * rows * weight.size, bytes_accessed=2 * weight.size, transcendentals=0
        ),
        name="project",
    )(table, normed, weight)


def slots_kernel(plan, table, packet, tokens, own, other):
    half = R_PF // 2
    size = packet.shape[2]
    for local in range(R_PF):
        target = own if local < half else other
        slot = (local + table[plan.parity] * half) % R_PF
        target[local % half, :, :size] = packet[table[plan.slot_place + slot]]
        target[local % half, :, size:] = tokens[slot]


def split_slots(plan, table, packet, tokens):
    shape = (R_PF // 2, 1, packet.shape[2] + tokens.shape[2])
    out = jax.ShapeDtypeStruct(shape, jnp.float32)
    return pl.pallas_call(
        functools.partial(slots_kernel, plan),
        grid_spec=pltpu.PrefetchScalarGridSpec(
            num_scalar_prefetch=1,
            grid=(1,),
            in_specs=[whole(packet), whole(tokens)],
            out_specs=[whole(out)] * 2,
        ),
        out_shape=[out, out],
        name="slots",
    )(table, packet, tokens)


def windows_kernel(plan, groups, conv_width, starts, table, own, got, out):
    parity = table[plan.parity]
    for owner, packet in enumerate((own, got)):
        side = jnp.where(parity == owner, 0, groups)
        for slot in range(R_PF // 2):
            for row, start in enumerate(starts):
                for group in range(groups):
                    first = start + group * conv_width
                    out[0, 0, slot, row, pl.ds(side + group, 1)] = packet[
                        slot, :, first : first + conv_width
                    ]


def write_windows(plan, table, own, got, groups, conv_width, starts):
    shape = (1, 1, R_PF // 2, len(starts), 2 * groups, conv_width)
    out = jax.ShapeDtypeStruct(shape, jnp.float32)
    return pl.pallas_call(
        functools.partial(windows_kernel, plan, groups, conv_width, starts),
        grid_spec=pltpu.PrefetchScalarGridSpec(
            num_scalar_prefetch=1,
            grid=(1,),
            in_specs=[whole(own), whole(got)],
            out_specs=whole(out),
        ),
        out_shape=out,
        name="windows",
    )(table, own, got)


def pack_kernel(count, cap, _rows, *refs):
    inputs, outputs = refs[:count], refs[-(count // cap) :]
    for place in range(count):
        outputs[place // cap][place % cap] = inputs[place][0].astype(jnp.bfloat16)


def pack_chunk(plan, table, ssm_state, chunk, width, after):
    count, cap = plan.places, plan.cap
    block = (1, width, P_SIZE, N)
    specs = [
        pl.BlockSpec(block, functools.partial(lambda i, rows, p: (rows[plan.row_of + p], chunk, 0, 0), p=p))
        for p in range(count)
    ]
    shape = (cap, width, P_SIZE, N)
    return pl.pallas_call(
        functools.partial(pack_kernel, count, cap),
        grid_spec=pltpu.PrefetchScalarGridSpec(
            num_scalar_prefetch=1,
            grid=(1,),
            in_specs=specs + [ANY] * len(after),
            out_specs=[pl.BlockSpec(shape, lambda i, rows: (0, 0, 0, 0))] * (count // cap),
        ),
        out_shape=[jax.ShapeDtypeStruct(shape, jnp.bfloat16)] * (count // cap),
        compiler_params=pltpu.CompilerParams(vmem_limit_bytes=VMEM_LIMIT),
        cost_estimate=pl.CostEstimate(
            flops=0, bytes_accessed=6 * count * width * P_SIZE * N, transcendentals=0
        ),
        name="pack",
    )(table, *([ssm_state] * count), *after)


def route_kernel(plan, sources, table, *refs):
    cap = plan.cap
    arrived, keep, give = refs[:sources], refs[-2], refs[-1]
    half = keep.shape[0]
    for index in range(2 * half):
        target = keep if index < half else give
        place = table[plan.split_place + index]
        for source in range(sources):

            @pl.when(place // cap == source)
            def _():
                target[index % half] = arrived[source][place % cap]


def route_chunk(plan, table, arrived, half, after):
    shape = (half,) + arrived[0].shape[1:]
    out = jax.ShapeDtypeStruct(shape, jnp.bfloat16)
    return pl.pallas_call(
        functools.partial(route_kernel, plan, len(arrived)),
        grid_spec=pltpu.PrefetchScalarGridSpec(
            num_scalar_prefetch=1,
            grid=(1,),
            in_specs=[whole(one) for one in arrived] + [ANY] * len(after),
            out_specs=[whole(out)] * 2,
        ),
        out_shape=[out, out],
        compiler_params=pltpu.CompilerParams(vmem_limit_bytes=VMEM_LIMIT),
        cost_estimate=pl.CostEstimate(
            flops=0, bytes_accessed=8 * half * arrived[0][0].size, transcendentals=0
        ),
        name="route",
    )(table, *arrived, *after)


def finish_kernel(plan, width, heads, base, table, decay, keep, got, *refs):
    parts, out, done = refs[:8], refs[-2], refs[-1]
    owner = pl.program_id(0)
    slots = keep.shape[0]
    done[...] = jnp.zeros_like(done)

    def stack(first, second, slot):
        rows = jnp.concatenate([first[slot], second[slot]], axis=0)
        high = rows.astype(jnp.bfloat16).astype(jnp.float32)
        return high, rows - high

    def fill(source, first_update, second_update, first_taps, second_taps):
        for slot in range(slots):
            update_high, update_low = stack(first_update, second_update, slot)
            taps_high, taps_low = stack(first_taps, second_taps, slot)
            updates = jnp.concatenate([update_high, update_low, update_high, update_low], axis=0)
            taps = jnp.concatenate([taps_high, taps_high, taps_low, taps_low], axis=0)
            added = lax.dot_general(
                updates.astype(jnp.bfloat16),
                taps.astype(jnp.bfloat16),
                (((0,), (0,)), ((), ())),
                preferred_element_type=jnp.float32,
            ).reshape(width, P_SIZE, N)
            for head in range(width):
                factor = decay[(owner * slots + slot) * heads + base + head]
                out[0, 0, slot, head] = (
                    factor * source[slot, head].astype(jnp.float32) + added[head]
                )

    pl.when(owner == 0)(lambda: fill(keep, *parts[:4]))
    pl.when(owner == 1)(lambda: fill(got, *parts[4:]))


def finish_chunk(plan, table, so_far, keep, got, decay, own, other, chunk, heads):
    slots, width = keep.shape[:2]
    per_half = heads // width
    span = width * P_SIZE
    channels = heads * P_SIZE
    groups = heads // PER_GROUP
    group = chunk * width // PER_GROUP
    taps_at = 2 * channels // N
    out_shape = jax.ShapeDtypeStruct((1, 1, slots, 2 * heads, P_SIZE, N), jnp.float32)
    extra = [] if so_far is None else [so_far]

    def part(size, place):
        return pl.BlockSpec((slots, 1, size), lambda o, t, d: (0, 0, place))

    parts = [
        part(span, chunk),
        part(span, channels // span + chunk),
        part(N, taps_at + group),
        part(N, taps_at + groups + group),
    ]
    side = lambda o, t: (o + t[plan.parity]) % 2
    return pl.pallas_call(
        functools.partial(finish_kernel, plan, width, heads, chunk * width),
        grid_spec=pltpu.PrefetchScalarGridSpec(
            num_scalar_prefetch=2,
            grid=(2,),
            in_specs=[whole(keep), whole(got)] + parts + parts + [ANY] * len(extra),
            out_specs=[
                pl.BlockSpec(
                    (1, 1, slots, width, P_SIZE, N),
                    lambda o, t, d: (0, 0, 0, side(o, t) * per_half + chunk, 0, 0),
                ),
                pl.BlockSpec((8, 128), lambda o, t, d: (0, 0)),
            ],
        ),
        out_shape=[out_shape, jax.ShapeDtypeStruct((8, 128), jnp.float32)],
        input_output_aliases={12: 0} if extra else {},
        compiler_params=pltpu.CompilerParams(vmem_limit_bytes=VMEM_LIMIT),
        cost_estimate=pl.CostEstimate(
            flops=64 * slots * width * P_SIZE * N,
            bytes_accessed=12 * slots * width * P_SIZE * N,
            transcendentals=0,
        ),
        name="finish",
    )(table, decay, keep, got, *([own] * 4), *([other] * 4), *extra)


def on_device(
    ssm_state,
    conv_state,
    counts,
    request_slot,
    token_xbc,
    token_z,
    token_dt,
    conv_weight,
    conv_bias,
    a_log,
    dt_bias,
    d_skip,
    norm_gain,
    out_weight,
):
    f32 = jnp.float32
    req_count = lax.axis_size("req")
    head_count = lax.axis_size("head")
    plan = Plan(req_count)
    slot_dev = R_PF // 2
    steps = token_xbc.shape[0]
    heads = ssm_state.shape[1]
    groups = conv_state.shape[2]
    conv_width = conv_state.shape[3]
    width = heads // CHUNKS
    channels = groups * X_WIDTH

    def swap(value):
        return lax.ppermute(value, "head", [(i, i ^ 1) for i in range(head_count)])

    def exchange(value):
        return lax.all_to_all(value, "req", split_axis=0, concat_axis=0, tiled=True)

    table = make_plan(plan, request_slot, counts)

    tokens = exchange(
        pack_tokens(plan, table, jnp.swapaxes(token_xbc, 1, 2), token_z, token_dt)
    )
    small = jnp.stack([a_log, dt_bias, d_skip]).astype(f32)
    normed, packet = run_rows(
        plan,
        table,
        tokens,
        jnp.moveaxis(conv_state, 0, 2),
        conv_weight,
        conv_bias,
        small,
        norm_gain.astype(f32)[None],
        ssm_state,
    )

    share = plan.rows // head_count
    projected = project(
        plan, share, table, lax.all_gather(normed, "req", axis=0, tiled=True), out_weight
    ).reshape(head_count, -1, out_weight.shape[1])
    layer_out = lax.psum_scatter(projected, "head", scatter_dimension=0, tiled=True)
    layer_out = layer_out.astype(jnp.bfloat16).reshape(steps, share, -1)

    local_tokens = jnp.swapaxes(token_xbc, 0, 1).reshape(R_PF, 1, -1).astype(f32)
    own, other = split_slots(plan, table, exchange(packet), local_tokens)
    other = swap(other)
    taps_at = steps * channels
    last_at = taps_at + steps * groups * N
    decay_at = last_at + groups * conv_width
    fresh_at = decay_at + LANES
    starts = [last_at] + [fresh_at + step * groups * conv_width for step in range(steps)]
    out_conv = write_windows(plan, table, own, other, groups, conv_width, starts)
    decay = jnp.stack([own, other])[:, :, 0, decay_at : decay_at + heads].reshape(-1)

    gives, gots, dones, out_ssm = [], [], [], None
    for chunk in range(CHUNKS):
        packed = pack_chunk(plan, table, ssm_state, chunk, width, gives[: chunk - AHEAD + 1][-1:])
        arrived = [packed[0]]
        for shift in range(1, req_count):
            pairs = [(i, i ^ shift) for i in range(req_count)]
            arrived.append(lax.ppermute(packed[shift], "req", pairs))
        keep, give = route_chunk(
            plan, table, arrived, slot_dev, gots[-1:] + dones[: chunk - 1][-1:]
        )
        gives.append(give)
        gots.append(swap(give))
        out_ssm, done = finish_chunk(
            plan, table, out_ssm, keep, gots[-1], decay, own, other, chunk, heads
        )
        dones.append(done)
    return (layer_out, out_ssm, out_conv)


def solution(mesh):
    in_specs = (
        P(("groups", "req"), "head", None, None),
        P(("groups", "req"), None, "head", None),
        P("groups"),
        P("groups"),
        P(None, ("groups", "req"), "head", None),
        P(None, ("groups", "req"), "head"),
        P(None, ("groups", "req"), "head"),
        P(None, "head", None),
        P("head", None),
        P("head"),
        P("head"),
        P("head"),
        P("head"),
        P("head", "req"),
    )
    out_specs = (
        P(None, ("groups", "head"), "req"),
        P(("groups", "req"), "head", None, None, None, None),
        P(("groups", "req"), "head", None, None, None, None),
    )
    return jax.shard_map(
        on_device, mesh=mesh, in_specs=in_specs, out_specs=out_specs, check_vma=False
    )
```

```python
import functools

import jax
import jax.numpy as jnp
from jax import lax
from jax.experimental import pallas as pl
from jax.experimental.pallas import tpu as pltpu
from jax.sharding import PartitionSpec as P

H = 128
P_SIZE = 64
N = 128
G = 8
R_PF = 8
PER_GROUP = H // G
X_WIDTH = PER_GROUP * P_SIZE
CHUNKS = ((0, 2), (2, 2), (4, 2), (6, 2))
UNITS = 8
NEAR = 2
ROWS = 2 * R_PF
PARTS = 4
LANES = 128
VMEM_LIMIT = 48 * 1024 * 1024
SCALE = 1.0


def cost(microseconds):
    return pl.CostEstimate(
        flops=0, bytes_accessed=int(SCALE * 3.2e6 * microseconds), transcendentals=0
    )


ANY = pl.BlockSpec(memory_space=pl.ANY)


def split_bf16(value):
    high = value.astype(jnp.bfloat16)
    low = (value - high.astype(jnp.float32)).astype(jnp.bfloat16)
    return high, low


class Plan:
    def __init__(self, req_count):
        self.cap = (R_PF + req_count - 1) // req_count
        self.places = req_count * self.cap
        self.rows = req_count * R_PF
        self.row_of = 0
        self.row_place = self.row_of + self.places
        self.slot_place = self.row_place + R_PF
        self.split_place = self.slot_place + R_PF
        self.live = self.split_place + R_PF
        self.parity = self.live + 1
        self.req = self.parity + 1
        self.head = self.req + 1
        self.slot_row = self.head + 1
        self.size = self.slot_row + self.rows


def plan_kernel(plan, request_slot, counts, out):
    me = lax.axis_index("req")
    parity = lax.axis_index("head") % 2
    half = R_PF // 2
    out[plan.live] = counts[me]
    out[plan.parity] = parity
    out[plan.req] = me
    out[plan.head] = lax.axis_index("head")
    for place in range(plan.places):
        out[plan.row_of + place] = 0

    dests = [request_slot[me * R_PF + row] // R_PF for row in range(R_PF)]
    for row in range(R_PF):
        rank = sum([(dests[row] == dests[other]).astype(jnp.int32) for other in range(row)], 0)
        out[plan.row_place + row] = dests[row] * plan.cap + rank
        out[plan.row_of + (dests[row] ^ me) * plan.cap + rank] = row

    @pl.loop(0, plan.rows // R_PF)
    def _(group):
        seen = jnp.int32(0)
        for row in range(R_PF):
            slot = request_slot[group * R_PF + row]
            out[plan.slot_row + slot] = group * R_PF + row
            here = slot // R_PF == me
            local = slot % R_PF

            @pl.when(here)
            def _():
                out[plan.slot_place + local] = group * plan.cap + seen
                out[plan.split_place + (local + parity * half) % R_PF] = (
                    group ^ me
                ) * plan.cap + seen

            seen = seen + here.astype(jnp.int32)


def make_plan(plan, request_slot, counts):
    smem = pl.BlockSpec(memory_space=pltpu.SMEM)
    return pl.pallas_call(
        functools.partial(plan_kernel, plan),
        in_specs=[smem, smem],
        out_specs=smem,
        out_shape=jax.ShapeDtypeStruct((plan.size,), jnp.int32),
        compiler_params=pltpu.CompilerParams(vmem_limit_bytes=VMEM_LIMIT),
        cost_estimate=cost(1.6),
        name="plan",
    )(request_slot, counts)


def one_hot(shape, pairs):
    rows = lax.broadcasted_iota(jnp.int32, shape, 0)
    columns = lax.broadcasted_iota(jnp.int32, shape, 1)
    total = jnp.zeros(shape, jnp.float32)
    for row, column in pairs:
        total = jnp.where((rows == row) & (columns == column), 1.0, total)
    return total.astype(jnp.bfloat16)


def pick(matrix, values):
    return jnp.dot(matrix, values, preferred_element_type=jnp.float32)


def tokens_kernel(plan, table, xbc, z, dt, *refs):
    out = refs[-1]
    steps, groups = xbc.shape[:2]
    matrix = one_hot(
        (plan.places, R_PF), [(table[plan.slot_place + slot], slot) for slot in range(R_PF)]
    )

    def put(values, start):
        picked = pick(matrix, values)
        size = values.shape[1]
        for source in range(plan.places // plan.cap):
            rows = picked[source * plan.cap : (source + 1) * plan.cap]
            out[source, :, start : start + size] = rows.astype(jnp.bfloat16)

    at = 0
    for step in range(steps):
        for group in range(groups):
            put(xbc[step, group], at)
            at += xbc.shape[3]
        put(z[step], at)
        at += z.shape[2]
        put(dt[step], at)
        at += LANES


def pack_tokens(plan, table, xbc, z, dt, after):
    steps, groups = xbc.shape[:2]
    size = steps * (groups * xbc.shape[3] + z.shape[2] + LANES)
    return pl.pallas_call(
        functools.partial(tokens_kernel, plan),
        grid_spec=pltpu.PrefetchScalarGridSpec(
            num_scalar_prefetch=1,
            grid=(1,),
            in_specs=[whole(xbc), whole(z), whole(dt)] + [ANY] * len(after),
            out_specs=pl.BlockSpec((plan.places // plan.cap, plan.cap, size), lambda i, t: (0, 0, 0)),
        ),
        out_shape=jax.ShapeDtypeStruct((plan.places // plan.cap, plan.cap, size), jnp.bfloat16),
        compiler_params=pltpu.CompilerParams(vmem_limit_bytes=VMEM_LIMIT),
        cost_estimate=cost(1.4),
        name="tokens",
    )(table, xbc, z, dt, *after)


def whole(array):
    return pl.BlockSpec(array.shape, lambda *_: (0,) * array.ndim)


def silu(value):
    return value / (1.0 + jnp.exp(-value))


def packet_places(groups, conv_width):
    taps_at = 2 * groups * X_WIDTH
    last_at = taps_at + 2 * groups * N
    decay_at = last_at + groups * conv_width
    return taps_at, last_at, decay_at, decay_at + LANES


def rows_kernel(plan, table, tokens, conv, weight, bias, small, gain, *refs):
    states = refs[:PARTS]
    out, read, read_taps, acts, wide, gates, lines = refs[-7:]
    steps = 2
    taps, groups, conv_width = weight.shape
    heads = states[0].shape[1] * PARTS
    channels = groups * X_WIDTH
    index = pl.program_id(0)
    row_ids = lax.broadcasted_iota(jnp.int32, (R_PF, 1), 0)
    live = row_ids < table[plan.live]
    f32, bf16 = jnp.float32, jnp.bfloat16
    taps_at, last_at, decay_at, _ = packet_places(groups, conv_width)

    @pl.when(index == 0)
    def _():
        matrix = one_hot(
            (R_PF, plan.places), [(row, table[plan.row_place + row]) for row in range(R_PF)]
        )
        stride = tokens.shape[2] // steps

        def rows_of(start, size):
            parts = [tokens[source, :, start : start + size] for source in range(tokens.shape[0])]
            parts = jnp.concatenate([part.astype(f32) for part in parts], axis=0)
            return pick(matrix, parts.astype(bf16))

        for group in range(groups):
            window = [
                jnp.where(live, conv[tap, group], 0.0) for tap in range(taps - 1)
            ] + [
                rows_of(step * stride + group * conv_width, conv_width) for step in range(steps)
            ]
            kernel = [weight[tap].astype(f32)[group : group + 1] for tap in range(taps)]
            offset = bias[...].astype(f32)[group : group + 1]
            parts = []
            for step in range(steps):
                total = sum(window[step + tap] * kernel[tap] for tap in range(taps)) + offset
                act = silu(total)
                acts[step, group] = act
                parts.append(act[:, X_WIDTH + N :])
            high = [part.astype(bf16).astype(f32) for part in parts]
            low = [part - near for part, near in zip(parts, high)]
            read_taps[group] = jnp.concatenate(high + low, axis=0).astype(bf16)
            start = last_at + group * conv_width
            lines[:, start : start + conv_width] = window[taps - 2]

        dts, decays = [], []
        rate = jnp.exp(small[0:1, :heads])
        for step in range(steps):
            base = step * stride + groups * conv_width
            gates[step] = silu(rows_of(base, channels))
            raw = rows_of(base + channels, LANES)[:, :heads] + small[1:2, :heads]
            dts.append(jnp.maximum(raw, 0.0) + jnp.log1p(jnp.exp(-jnp.abs(raw))))
            decays.append(jnp.exp(-dts[-1] * rate))
        lines[:, decay_at : decay_at + LANES] = jnp.concatenate(
            [jnp.where(live, decays[0] * decays[1], 0.0), jnp.zeros((R_PF, LANES - heads), f32)],
            axis=1,
        )
        skip = jnp.broadcast_to(small[2:3, :heads], (R_PF, heads))
        narrow = jnp.concatenate(dts + decays + [skip], axis=0)
        high = narrow.astype(bf16).astype(f32)
        middle = (narrow - high).astype(bf16).astype(f32)
        narrow = jnp.concatenate([high, middle, narrow - high - middle], axis=1).astype(bf16)
        head_ids = lax.broadcasted_iota(jnp.int32, (3 * heads, channels), 0) % heads
        channel_ids = lax.broadcasted_iota(jnp.int32, (3 * heads, channels), 1) // P_SIZE
        spread = pick(narrow, (head_ids == channel_ids).astype(bf16))
        for part in range(5):
            wide[part] = spread[part * R_PF : (part + 1) * R_PF]

    for part, state in enumerate(states):
        size = heads // PARTS * P_SIZE
        group, start = part * size // X_WIDTH, part * size % X_WIDTH
        state_high, state_low = split_bf16(state[0].reshape(size, N))
        dims = (((1,), (1,)), ((), ()))
        total = lax.dot_general(read_taps[group], state_high, dims, preferred_element_type=f32)
        rest = lax.dot_general(
            read_taps[group, : steps * R_PF], state_low, dims, preferred_element_type=f32
        )
        total = total[: steps * R_PF] + total[steps * R_PF :] + rest
        for step in range(steps):
            now = total[step * R_PF : (step + 1) * R_PF]
            span = slice(start, start + size)
            read[group, step, :, span] = jnp.where(row_ids == index, now, read[group, step, :, span])

    @pl.when(index == R_PF - 1)
    def _():
        for group in range(groups):
            span = slice(group * X_WIDTH, (group + 1) * X_WIDTH)
            x = [acts[step, group, :, :X_WIDTH] for step in range(steps)]
            b = [acts[step, group, :, X_WIDTH : X_WIDTH + N] for step in range(steps)]
            c = [acts[step, group, :, X_WIDTH + N :] for step in range(steps)]
            u = [wide[step, :, span] * x[step] for step in range(steps)]
            first_decay, second_decay, skip = wide[2, :, span], wide[3, :, span], wide[4, :, span]
            held = [jnp.where(live, read[group, step], 0.0) for step in range(steps)]

            def pair_sum(one, two):
                return jnp.sum(one * two, axis=1, keepdims=True)

            later = second_decay * u[0]
            y = [
                first_decay * held[0] + pair_sum(b[0], c[0]) * u[0] + skip * x[0],
                second_decay * first_decay * held[1]
                + pair_sum(b[0], c[1]) * later
                + pair_sum(b[1], c[1]) * u[1]
                + skip * x[1],
            ]
            result = []
            for step in range(steps):
                gated = y[step] * gates[step, :, span]
                scale = lax.rsqrt(jnp.mean(gated * gated, axis=1, keepdims=True) + 1e-05)
                result.append(gated * scale * gain[0:1, span])
            together = jnp.concatenate(result, axis=0).astype(bf16)
            for target in range(out.shape[0]):
                out[target, :ROWS, span] = together
            lines[:, span] = later
            lines[:, channels + group * X_WIDTH : channels + (group + 1) * X_WIDTH] = u[1]
            for step in range(steps):
                start = taps_at + (step * groups + group) * N
                lines[:, start : start + N] = b[step]
        segments = lines.shape[1] // channels
        values = [lines[:, part * channels : (part + 1) * channels] for part in range(segments)]
        high = [value.astype(bf16).astype(f32) for value in values]
        low = [value - near for value, near in zip(values, high)]
        pairs = []
        for row in range(R_PF):
            place = table[plan.row_place + row]
            first = place // plan.cap * ROWS + place % plan.cap * 2 * segments
            pairs += [(first + part, part * R_PF + row) for part in range(2 * segments)]
        matrix = one_hot((out.shape[0] * ROWS, 2 * segments * R_PF), pairs)
        placed = pick(matrix, jnp.concatenate(high + low, axis=0).astype(bf16)).astype(bf16)
        for target in range(out.shape[0]):
            out[target, ROWS:] = placed[target * ROWS : (target + 1) * ROWS]


def run_rows(plan, table, tokens, conv, weight, bias, small, gain, ssm_state, after):
    taps, groups, conv_width = weight.shape
    steps = 2
    heads = ssm_state.shape[1]
    sources = plan.places // plan.cap
    channels = groups * X_WIDTH
    size = -(-packet_places(groups, conv_width)[-1] // channels) * channels
    f32 = jnp.float32
    return pl.pallas_call(
        functools.partial(rows_kernel, plan),
        grid_spec=pltpu.PrefetchScalarGridSpec(
            num_scalar_prefetch=1,
            grid=(R_PF,),
            in_specs=[
                whole(tokens),
                whole(conv),
                whole(weight),
                whole(bias),
                whole(small),
                whole(gain),
            ]
            + [
                pl.BlockSpec(
                    (1, heads // PARTS, P_SIZE, N),
                    functools.partial(lambda i, t, part: (i, part, 0, 0), part=part),
                )
                for part in range(PARTS)
            ]
            + [ANY] * len(after),
            out_specs=pl.BlockSpec((sources, 2 * ROWS, channels), lambda i, t: (0, 0, 0)),
            scratch_shapes=[
                pltpu.VMEM((groups, steps, R_PF, X_WIDTH), f32),
                pltpu.VMEM((groups, 2 * steps * R_PF, N), jnp.bfloat16),
                pltpu.VMEM((steps, groups, R_PF, conv_width), f32),
                pltpu.VMEM((5, R_PF, channels), f32),
                pltpu.VMEM((steps, R_PF, channels), f32),
                pltpu.VMEM((R_PF, size), f32),
            ],
        ),
        out_shape=jax.ShapeDtypeStruct((sources, 2 * ROWS, channels), jnp.bfloat16),
        compiler_params=pltpu.CompilerParams(vmem_limit_bytes=VMEM_LIMIT),
        cost_estimate=cost(9),
        name="rows",
    )(table, tokens, conv, weight, bias, small, gain, *([ssm_state] * PARTS), *after)


def project_kernel(plan, share, table, *refs):
    steps = 2
    targets = plan.rows // share
    normed, weights = refs[0], refs[1 : 1 + PARTS]
    own, out, picked = refs[-3:]

    @pl.when(pl.program_id(0) == 0)
    def _():
        shape = (steps * plan.rows, steps * plan.rows)
        rows = lax.broadcasted_iota(jnp.int32, shape, 0)
        columns = lax.broadcasted_iota(jnp.int32, shape, 1)

        def add(slot, total):
            row = table[plan.slot_row + slot]
            target = slot // share * steps * share + slot % share
            source = (row // R_PF) * steps * R_PF + row % R_PF
            for step in range(steps):
                hit = (rows == target + step * share) & (columns == source + step * R_PF)
                total = jnp.where(hit, 1.0, total)
            return total

        matrix = lax.fori_loop(0, plan.rows, add, jnp.zeros(shape, jnp.float32), unroll=8)
        matrix = matrix.astype(jnp.bfloat16)
        values = normed[...].reshape(picked.shape)
        picked[...] = pick(matrix, values).astype(jnp.bfloat16)

    depth = weights[0].shape[0]
    total = sum(
        pick(picked[:, part * depth : (part + 1) * depth], weights[part][...])
        for part in range(PARTS)
    )
    for target in range(targets):
        part = total[target * steps * share : (target + 1) * steps * share]
        out[target] = part.astype(out.dtype)

        @pl.when(table[plan.head] == target)
        def _():
            own[...] = part


def project(plan, share, table, normed, weight, after):
    depth = weight.shape[0]
    columns = weight.shape[1]
    block = min(512, columns)
    rows = 2 * share
    targets = plan.rows // share
    return pl.pallas_call(
        functools.partial(project_kernel, plan, share),
        grid_spec=pltpu.PrefetchScalarGridSpec(
            num_scalar_prefetch=1,
            grid=(columns // block,),
            in_specs=[pl.BlockSpec((normed.shape[0], ROWS, depth), lambda i, t: (0, 0, 0))]
            + [
                pl.BlockSpec(
                    (depth // PARTS, block), functools.partial(lambda i, t, part: (part, i), part=part)
                )
                for part in range(PARTS)
            ]
            + [ANY] * len(after),
            out_specs=[
                pl.BlockSpec((rows, block), lambda i, t: (0, i)),
                pl.BlockSpec((targets, rows, block), lambda i, t: (0, 0, i)),
            ],
            scratch_shapes=[pltpu.VMEM((2 * plan.rows, depth), jnp.bfloat16)],
        ),
        out_shape=[
            jax.ShapeDtypeStruct((rows, columns), jnp.float32),
            jax.ShapeDtypeStruct((targets, rows, columns), jnp.bfloat16),
        ],
        compiler_params=pltpu.CompilerParams(vmem_limit_bytes=VMEM_LIMIT),
        cost_estimate=cost(6),
        name="project",
    )(table, normed, *([weight] * PARTS), *after)


def slots_kernel(plan, decay_at, table, packets, xbc, *refs):
    own, other = refs[-2:]
    f32, bf16 = jnp.float32, jnp.bfloat16
    steps, groups = xbc.shape[:2]
    half = R_PF // 2
    sources, _, channels = packets.shape
    segments = (own.shape[1] - LANES - steps * groups * xbc.shape[3]) // channels
    pairs, order = [], []
    for local in range(R_PF):
        slot = (local + table[plan.parity] * half) % R_PF
        order.append((local, slot))
        place = table[plan.slot_place + slot]
        first = place // plan.cap * ROWS + place % plan.cap * 2 * segments
        pairs += [(part * R_PF + local, first + part) for part in range(2 * segments)]
    matrix = one_hot((2 * segments * R_PF, sources * ROWS), pairs)
    order = one_hot((R_PF, R_PF), order)

    def put(values, start):
        size = values.shape[1]
        own[:, start : start + size] = values[:half].astype(bf16)
        other[:, start : start + size] = values[half:].astype(bf16)

    picked = pick(matrix, packets[...].reshape(sources * ROWS, channels))
    for part in range(segments):
        high = picked[part * R_PF : (part + 1) * R_PF]
        low = picked[(segments + part) * R_PF : (segments + part + 1) * R_PF]
        put(high + low, part * channels)
        if decay_at // channels == part:
            span = slice(decay_at % channels, decay_at % channels + LANES)
            put(low[:, span], segments * channels)
    at = segments * channels + LANES
    for step in range(steps):
        for group in range(groups):
            put(pick(order, xbc[step, group]), at)
            at += xbc.shape[3]


def split_slots(plan, table, packets, xbc, after):
    steps, groups, _, conv_width = xbc.shape
    sources, _, channels = packets.shape
    decay_at, end = packet_places(groups, conv_width)[2:]
    size = -(-end // channels) * channels + LANES + steps * groups * conv_width
    out = jax.ShapeDtypeStruct((R_PF // 2, size), jnp.bfloat16)
    return pl.pallas_call(
        functools.partial(slots_kernel, plan, decay_at),
        grid_spec=pltpu.PrefetchScalarGridSpec(
            num_scalar_prefetch=1,
            grid=(1,),
            in_specs=[
                pl.BlockSpec((sources, ROWS, channels), lambda i, t: (0, 1, 0)),
                whole(xbc),
            ]
            + [ANY] * len(after),
            out_specs=[whole(out)] * 2,
        ),
        out_shape=[out, out],
        compiler_params=pltpu.CompilerParams(vmem_limit_bytes=VMEM_LIMIT),
        cost_estimate=cost(1),
        name="slots",
    )(table, packets, xbc, *after)


def windows_kernel(plan, groups, conv_width, starts, table, own, got, out):
    parity = table[plan.parity]
    for owner, packet in enumerate((own, got)):
        side = jnp.where(parity == owner, 0, groups)
        for row, start in enumerate(starts):
            for group in range(groups):
                first = start + group * conv_width
                values = packet[:, first : first + conv_width].astype(jnp.float32)
                for slot in range(R_PF // 2):
                    out[0, 0, slot, row, pl.ds(side + group, 1)] = values[slot : slot + 1]


def write_windows(plan, table, own, got, groups, conv_width, starts):
    shape = (1, 1, R_PF // 2, len(starts), 2 * groups, conv_width)
    out = jax.ShapeDtypeStruct(shape, jnp.float32)
    return pl.pallas_call(
        functools.partial(windows_kernel, plan, groups, conv_width, starts),
        grid_spec=pltpu.PrefetchScalarGridSpec(
            num_scalar_prefetch=1,
            grid=(1,),
            in_specs=[whole(own), whole(got)],
            out_specs=whole(out),
        ),
        out_shape=out,
        compiler_params=pltpu.CompilerParams(vmem_limit_bytes=VMEM_LIMIT),
        cost_estimate=cost(1.3),
        name="windows",
    )(table, own, got)


def pack_kernel(count, cap, _table, *refs):
    inputs, outputs = refs[:count], refs[-(count // cap) :]
    for place in range(count):
        outputs[place // cap][place % cap] = inputs[place][0].astype(jnp.bfloat16)


def pack_rows(plan, table, ssm_state, shifts, first, width, cuts, after):
    cap = plan.cap
    places = [shift * cap + rank for shift in shifts for rank in range(cap)]
    piece = width // cuts
    start = first // piece
    specs = [
        pl.BlockSpec(
            (1, piece, P_SIZE, N),
            functools.partial(
                lambda i, rows, place: (rows[plan.row_of + place], start + i, 0, 0), place=place
            ),
        )
        for place in places
    ]
    out = jax.ShapeDtypeStruct((cap, width, P_SIZE, N), jnp.bfloat16)
    return pl.pallas_call(
        functools.partial(pack_kernel, len(places), cap),
        grid_spec=pltpu.PrefetchScalarGridSpec(
            num_scalar_prefetch=1,
            grid=(cuts,),
            in_specs=specs + [ANY] * len(after),
            out_specs=[pl.BlockSpec((cap, piece, P_SIZE, N), lambda i, rows: (0, i, 0, 0))]
            * len(shifts),
        ),
        out_shape=[out] * len(shifts),
        compiler_params=pltpu.CompilerParams(vmem_limit_bytes=VMEM_LIMIT),
        cost_estimate=cost(2.5),
        name=f"pack_{first}_{width}",
    )(table, *([ssm_state] * len(places)), *after)


def route_kernel(plan, sources, table, *refs):
    cap = plan.cap
    arrived, keep, give = refs[:sources], refs[-2], refs[-1]
    half = keep.shape[0]
    for index in range(2 * half):
        target = keep if index < half else give
        place = table[plan.split_place + index]
        for source in range(sources):

            @pl.when(place // cap == source)
            def _():
                target[index % half] = arrived[source][place % cap]


def route_chunk(plan, table, near, far, first, after):
    width = far[0].shape[1]
    half = R_PF // 2
    out = jax.ShapeDtypeStruct((half, width, P_SIZE, N), jnp.bfloat16)
    block = pl.BlockSpec((plan.cap, width, P_SIZE, N), lambda i, rows: (0, first // width - 1, 0, 0))
    return pl.pallas_call(
        functools.partial(route_kernel, plan, len(near) + len(far)),
        grid_spec=pltpu.PrefetchScalarGridSpec(
            num_scalar_prefetch=1,
            grid=(1,),
            in_specs=[block] * len(near) + [whole(one) for one in far] + [ANY] * len(after),
            out_specs=[whole(out)] * 2,
        ),
        out_shape=[out, out],
        compiler_params=pltpu.CompilerParams(vmem_limit_bytes=VMEM_LIMIT),
        cost_estimate=cost(1),
        name=f"route_{first}_{width}",
    )(table, *near, *far, *after)


def finish_kernel(plan, width, heads, base, table, decay, keep, got, *refs):
    parts, out, done = refs[:8], refs[-2], refs[-1]
    owner = pl.program_id(0)
    slots = keep.shape[0]
    done[...] = jnp.zeros_like(done)

    def fill(source, *pieces):
        first_update, second_update, first_taps, second_taps = [
            piece[...].astype(jnp.float32) for piece in pieces
        ]

        def stack(first, second, slot):
            blank = jnp.zeros((6, first.shape[1]), jnp.float32)
            rows = [first[slot : slot + 1], second[slot : slot + 1], blank]
            return jnp.concatenate(rows, axis=0).astype(jnp.bfloat16)

        for slot in range(slots):
            added = lax.dot_general(
                stack(first_update, second_update, slot),
                stack(first_taps, second_taps, slot),
                (((0,), (0,)), ((), ())),
                preferred_element_type=jnp.float32,
            ).reshape(width, P_SIZE, N)
            for head in range(width):
                factor = decay[(owner * slots + slot) * heads + base + head]
                out[0, 0, slot, head] = (
                    factor * source[slot, head].astype(jnp.float32) + added[head]
                )

    pl.when(owner == 0)(lambda: fill(keep, *parts[:4]))
    pl.when(owner == 1)(lambda: fill(got, *parts[4:]))


def finish_chunk(plan, table, so_far, keep, got, decay, own, other, first, heads):
    slots, width = keep.shape[:2]
    per_half = heads // width
    span = width * P_SIZE
    channels = heads * P_SIZE
    groups = heads // PER_GROUP
    group = first // PER_GROUP
    chunk = first // width
    taps_at = 2 * channels // N
    out_shape = jax.ShapeDtypeStruct((1, 1, slots, 2 * heads, P_SIZE, N), jnp.float32)
    extra = [] if so_far is None else [so_far]

    def part(size, place):
        return pl.BlockSpec((slots, size), lambda o, t, d: (0, place))

    parts = [
        part(span, chunk),
        part(span, channels // span + chunk),
        part(N, taps_at + group),
        part(N, taps_at + groups + group),
    ]
    side = lambda o, t: (o + t[plan.parity]) % 2
    return pl.pallas_call(
        functools.partial(finish_kernel, plan, width, heads, first),
        grid_spec=pltpu.PrefetchScalarGridSpec(
            num_scalar_prefetch=2,
            grid=(2,),
            in_specs=[whole(keep), whole(got)] + parts + parts + [ANY] * len(extra),
            out_specs=[
                pl.BlockSpec(
                    (1, 1, slots, width, P_SIZE, N),
                    lambda o, t, d: (0, 0, 0, side(o, t) * per_half + chunk, 0, 0),
                ),
                pl.BlockSpec((8, 128), lambda o, t, d: (0, 0)),
            ],
        ),
        out_shape=[out_shape, jax.ShapeDtypeStruct((8, 128), jnp.float32)],
        input_output_aliases={12: 0} if extra else {},
        compiler_params=pltpu.CompilerParams(vmem_limit_bytes=VMEM_LIMIT),
        cost_estimate=cost(2.4),
        name=f"finish_{first}_{width}",
    )(table, decay, keep, got, *([own] * 4), *([other] * 4), *extra)


def on_device(
    ssm_state,
    conv_state,
    counts,
    request_slot,
    token_xbc,
    token_z,
    token_dt,
    conv_weight,
    conv_bias,
    a_log,
    dt_bias,
    d_skip,
    norm_gain,
    out_weight,
):
    f32 = jnp.float32
    req_count = lax.axis_size("req")
    head_count = lax.axis_size("head")
    plan = Plan(req_count)
    steps = token_xbc.shape[0]
    heads = ssm_state.shape[1]
    groups = conv_state.shape[2]
    conv_width = conv_state.shape[3]
    channels = groups * X_WIDTH

    def shifted(value, axis, shift):
        return lax.ppermute(value, axis, [(i, i ^ shift) for i in range(lax.axis_size(axis))])

    def swap(value):
        return shifted(value, "head", 1)

    def exchange(value, axis):
        return lax.all_to_all(value, axis, split_axis=0, concat_axis=0, tiled=True)

    table = make_plan(plan, request_slot, counts)

    unit = heads // UNITS
    count = len(CHUNKS)
    firsts = [start * unit for start, _ in CHUNKS]
    far, sent = [None] * count, [None] * count
    keeps, gives, gots = [None] * count, [None] * count, [None] * count

    def send(chunk, shifts, after):
        width = CHUNKS[chunk][1] * unit
        packed = pack_rows(plan, table, ssm_state, shifts, firsts[chunk], width, 2, after)
        sent[chunk] = packed[0]
        return [shifted(part, "req", shift) if shift else part for part, shift in zip(packed, shifts)]

    def route(chunk, near, far, after):
        keeps[chunk], gives[chunk] = route_chunk(plan, table, near, far, firsts[chunk], after)
        gots[chunk] = swap(gives[chunk])

    xbc = jnp.swapaxes(token_xbc, 1, 2)
    all_shifts, far_shifts = range(req_count), range(NEAR, req_count)
    far[0] = send(0, all_shifts, [])
    packed_tokens = pack_tokens(plan, table, xbc, token_z, token_dt, [sent[0]])
    tokens = exchange(packed_tokens, "req")
    far[1] = send(1, far_shifts, [packed_tokens])
    route(0, [], far[0], [sent[1], tokens])
    rest = UNITS - CHUNKS[0][1]
    near = pack_rows(
        plan, table, ssm_state, range(NEAR), CHUNKS[0][1] * unit, rest * unit, 3, [gives[0]]
    )
    far[2] = send(2, far_shifts, [gives[0]])
    near = [near[0]] + [shifted(near[shift], "req", shift) for shift in range(1, NEAR)]

    small = jnp.stack([a_log, dt_bias, d_skip]).astype(f32)
    result = run_rows(
        plan,
        table,
        tokens,
        jnp.moveaxis(conv_state, 0, 2),
        conv_weight,
        conv_bias,
        small,
        norm_gain.astype(f32)[None],
        ssm_state,
        [gives[0]],
    )
    route(1, near, far[1], [result, sent[2], gots[0]])
    far[3] = send(3, far_shifts, [gives[1]])
    result = exchange(result, "req")
    route(2, near, far[2], [sent[3], result, gots[1]])

    share = plan.rows // head_count
    own_sum, sums = project(plan, share, table, result, out_weight, [gives[2]])
    others = exchange(sums, "head").astype(f32)
    is_mine = jnp.arange(head_count) == lax.axis_index("head")
    layer_out = own_sum + jnp.sum(jnp.where(is_mine[:, None, None], 0.0, others), axis=0)
    layer_out = layer_out.astype(jnp.bfloat16).reshape(steps, share, -1)

    own, give = split_slots(plan, table, result, xbc, [gives[2]])
    other = swap(give)
    _, last_at, decay_at, end = packet_places(groups, conv_width)
    low_at = -(-end // channels) * channels
    fresh_at = low_at + LANES
    starts = [last_at] + [fresh_at + step * groups * conv_width for step in range(steps)]
    out_conv = write_windows(plan, table, own, other, groups, conv_width, starts)
    both = jnp.stack([own, other]).astype(f32)
    decay = both[:, :, decay_at : decay_at + heads] + both[:, :, low_at : low_at + heads]
    decay = decay.reshape(-1)
    route(3, near, far[3], [gots[2], sums, give])

    out_ssm = None
    for chunk in range(count):
        out_ssm, done = finish_chunk(
            plan, table, out_ssm, keeps[chunk], gots[chunk], decay, own, other, firsts[chunk], heads
        )
    return (layer_out, out_ssm, out_conv)


def solution(mesh):
    in_specs = (
        P(("groups", "req"), "head", None, None),
        P(("groups", "req"), None, "head", None),
        P("groups"),
        P("groups"),
        P(None, ("groups", "req"), "head", None),
        P(None, ("groups", "req"), "head"),
        P(None, ("groups", "req"), "head"),
        P(None, "head", None),
        P("head", None),
        P("head"),
        P("head"),
        P("head"),
        P("head"),
        P("head", "req"),
    )
    out_specs = (
        P(None, ("groups", "head"), "req"),
        P(("groups", "req"), "head", None, None, None, None),
        P(("groups", "req"), "head", None, None, None, None),
    )
    return jax.shard_map(
        on_device, mesh=mesh, in_specs=in_specs, out_specs=out_specs, check_vma=False
    )
```

```python
import functools

import jax
import jax.numpy as jnp
from jax import lax
from jax.experimental import pallas as pl
from jax.experimental.pallas import tpu as pltpu
from jax.sharding import PartitionSpec as P

H = 128
P_SIZE = 64
N = 128
G = 8
R_PF = 8
PER_GROUP = H // G
X_WIDTH = PER_GROUP * P_SIZE
CHUNKS = ((0, 2), (2, 2), (4, 2), (6, 2))
UNITS = 8
NEAR = 2
ROWS = 2 * R_PF
PARTS = 4
BLOCKS = 8
LANES = 128
VMEM_LIMIT = 48 * 1024 * 1024
VMEM_LARGE = 48 * 1024 * 1024
ANY = pl.BlockSpec(memory_space=pl.ANY)
HBM = pl.BlockSpec(memory_space=pltpu.HBM)


def split_bf16(value):
    high = value.astype(jnp.bfloat16)
    low = (value - high.astype(jnp.float32)).astype(jnp.bfloat16)
    return high, low


class Plan:
    def __init__(self, req_count):
        self.cap = (R_PF + req_count - 1) // req_count
        self.places = req_count * self.cap
        self.rows = req_count * R_PF
        self.row_of = 0
        self.row_place = self.row_of + self.places
        self.slot_place = self.row_place + R_PF
        self.split_place = self.slot_place + R_PF
        self.live = self.split_place + R_PF
        self.parity = self.live + 1
        self.req = self.parity + 1
        self.head = self.req + 1
        self.slot_row = self.head + 1
        self.size = self.slot_row + self.rows


def plan_kernel(plan, request_slot, counts, out):
    me = lax.axis_index("req")
    parity = lax.axis_index("head") % 2
    half = R_PF // 2
    out[plan.live] = counts[me]
    out[plan.parity] = parity
    out[plan.req] = me
    out[plan.head] = lax.axis_index("head")
    for place in range(plan.places):
        out[plan.row_of + place] = 0

    dests = [request_slot[me * R_PF + row] // R_PF for row in range(R_PF)]
    for row in range(R_PF):
        rank = sum([(dests[row] == dests[other]).astype(jnp.int32) for other in range(row)], 0)
        out[plan.row_place + row] = dests[row] * plan.cap + rank
        out[plan.row_of + (dests[row] ^ me) * plan.cap + rank] = row

    @pl.loop(0, plan.rows // R_PF)
    def _(group):
        seen = jnp.int32(0)
        for row in range(R_PF):
            slot = request_slot[group * R_PF + row]
            out[plan.slot_row + slot] = group * R_PF + row
            here = slot // R_PF == me
            local = slot % R_PF

            @pl.when(here)
            def _():
                out[plan.slot_place + local] = group * plan.cap + seen
                out[plan.split_place + (local + parity * half) % R_PF] = (
                    group ^ me
                ) * plan.cap + seen

            seen = seen + here.astype(jnp.int32)


def make_plan(plan, request_slot, counts):
    smem = pl.BlockSpec(memory_space=pltpu.SMEM)
    return pl.pallas_call(
        functools.partial(plan_kernel, plan),
        in_specs=[smem, smem],
        out_specs=smem,
        out_shape=jax.ShapeDtypeStruct((plan.size,), jnp.int32),
        compiler_params=pltpu.CompilerParams(vmem_limit_bytes=VMEM_LIMIT),
        name="plan",
    )(request_slot, counts)


def one_hot(shape, pairs):
    rows = lax.broadcasted_iota(jnp.int32, shape, 0)
    columns = lax.broadcasted_iota(jnp.int32, shape, 1)
    total = jnp.zeros(shape, jnp.float32)
    for row, column in pairs:
        total = jnp.where((rows == row) & (columns == column), 1.0, total)
    return total.astype(jnp.bfloat16)


def pick(matrix, values):
    return jnp.dot(matrix, values, preferred_element_type=jnp.float32)


def tokens_kernel(plan, table, xbc, z, dt, *refs):
    out = refs[-1]
    steps, groups = xbc.shape[:2]
    matrix = one_hot(
        (plan.places, R_PF), [(table[plan.slot_place + slot], slot) for slot in range(R_PF)]
    )

    def put(values, start):
        picked = pick(matrix, values)
        size = values.shape[1]
        for source in range(plan.places // plan.cap):
            rows = picked[source * plan.cap : (source + 1) * plan.cap]
            out[source, :, start : start + size] = rows.astype(jnp.bfloat16)

    at = 0
    for step in range(steps):
        for group in range(groups):
            put(xbc[step, group], at)
            at += xbc.shape[3]
        put(z[step], at)
        at += z.shape[2]
        put(dt[step], at)
        at += LANES


def pack_tokens(plan, table, xbc, z, dt, after):
    steps, groups = xbc.shape[:2]
    size = steps * (groups * xbc.shape[3] + z.shape[2] + LANES)
    return pl.pallas_call(
        functools.partial(tokens_kernel, plan),
        grid_spec=pltpu.PrefetchScalarGridSpec(
            num_scalar_prefetch=1,
            grid=(1,),
            in_specs=[whole(xbc), whole(z), whole(dt)] + [ANY] * len(after),
            out_specs=pl.BlockSpec((plan.places // plan.cap, plan.cap, size), lambda i, t: (0, 0, 0)),
        ),
        out_shape=jax.ShapeDtypeStruct((plan.places // plan.cap, plan.cap, size), jnp.bfloat16),
        compiler_params=pltpu.CompilerParams(vmem_limit_bytes=VMEM_LIMIT),
        name="tokens",
    )(table, xbc, z, dt, *after)


def whole(array):
    return pl.BlockSpec(array.shape, lambda *_: (0,) * array.ndim)


def silu(value):
    return value / (1.0 + jnp.exp(-value))


def packet_places(groups, conv_width):
    taps_at = 2 * groups * X_WIDTH
    last_at = taps_at + 2 * groups * N
    decay_at = last_at + groups * conv_width
    return taps_at, last_at, decay_at, decay_at + LANES


def rows_kernel(plan, table, tokens, conv, weight, bias, small, gain, state, *refs):
    out, states, sems, read, read_taps, acts, wide, gates, lines = refs[-9:]
    steps = 2
    taps, groups, conv_width = weight.shape
    heads = state.shape[1]
    channels = groups * X_WIDTH
    row_ids = lax.broadcasted_iota(jnp.int32, (R_PF, 1), 0)
    live = row_ids < table[plan.live]
    f32, bf16 = jnp.float32, jnp.bfloat16
    taps_at, last_at, decay_at, _ = packet_places(groups, conv_width)

    share = heads // PARTS

    def copy(row, part):
        span = pl.ds(part * share, share)
        return pltpu.make_async_copy(
            state.at[row, span], states.at[row, span], sems.at[row * PARTS + part]
        )

    for row in range(R_PF):
        for part in range(PARTS):
            copy(row, part).start()

    matrix = one_hot(
        (R_PF, plan.places), [(row, table[plan.row_place + row]) for row in range(R_PF)]
    )
    stride = tokens.shape[2] // steps

    def rows_of(start, size):
        parts = [tokens[source, :, start : start + size] for source in range(tokens.shape[0])]
        parts = jnp.concatenate([part.astype(f32) for part in parts], axis=0)
        return pick(matrix, parts.astype(bf16))

    for group in range(groups):
        window = [
            jnp.where(live, conv[tap, group], 0.0) for tap in range(taps - 1)
        ] + [
            rows_of(step * stride + group * conv_width, conv_width) for step in range(steps)
        ]
        kernel = [weight[tap].astype(f32)[group : group + 1] for tap in range(taps)]
        offset = bias[...].astype(f32)[group : group + 1]
        parts = []
        for step in range(steps):
            total = sum(window[step + tap] * kernel[tap] for tap in range(taps)) + offset
            act = silu(total)
            acts[step, group] = act
            parts.append(act[:, X_WIDTH + N :])
        high = [part.astype(bf16).astype(f32) for part in parts]
        low = [part - near for part, near in zip(parts, high)]
        read_taps[group] = jnp.concatenate(high + low, axis=0).astype(bf16)
        start = last_at + group * conv_width
        lines[:, start : start + conv_width] = window[taps - 2]

    dts, decays = [], []
    rate = jnp.exp(small[0:1, :heads])
    for step in range(steps):
        base = step * stride + groups * conv_width
        gates[step] = silu(rows_of(base, channels))
        raw = rows_of(base + channels, LANES)[:, :heads] + small[1:2, :heads]
        dts.append(jnp.maximum(raw, 0.0) + jnp.log1p(jnp.exp(-jnp.abs(raw))))
        decays.append(jnp.exp(-dts[-1] * rate))
    lines[:, decay_at : decay_at + LANES] = jnp.concatenate(
        [jnp.where(live, decays[0] * decays[1], 0.0), jnp.zeros((R_PF, LANES - heads), f32)],
        axis=1,
    )
    skip = jnp.broadcast_to(small[2:3, :heads], (R_PF, heads))
    narrow = jnp.concatenate(dts + decays + [skip], axis=0)
    high = narrow.astype(bf16).astype(f32)
    middle = (narrow - high).astype(bf16).astype(f32)
    narrow = jnp.concatenate([high, middle, narrow - high - middle], axis=1).astype(bf16)
    head_ids = lax.broadcasted_iota(jnp.int32, (3 * heads, channels), 0) % heads
    channel_ids = lax.broadcasted_iota(jnp.int32, (3 * heads, channels), 1) // P_SIZE
    spread = pick(narrow, (head_ids == channel_ids).astype(bf16))
    for part in range(5):
        wide[part] = spread[part * R_PF : (part + 1) * R_PF]

    @pl.loop(0, R_PF)
    def _(index):
        for part in range(PARTS):
            copy(index, part).wait()
            size = share * P_SIZE
            group, start = part * size // X_WIDTH, part * size % X_WIDTH
            rows = states[index, part * share : (part + 1) * share].reshape(size, N)
            state_high, state_low = split_bf16(rows)
            dims = (((1,), (1,)), ((), ()))
            total = lax.dot_general(read_taps[group], state_high, dims, preferred_element_type=f32)
            rest = lax.dot_general(
                read_taps[group, : steps * R_PF], state_low, dims, preferred_element_type=f32
            )
            total = total[: steps * R_PF] + total[steps * R_PF :] + rest
            for step in range(steps):
                now = total[step * R_PF : (step + 1) * R_PF]
                span = slice(start, start + size)
                read[group, step, :, span] = jnp.where(
                    row_ids == index, now, read[group, step, :, span]
                )

    for group in range(groups):
        span = slice(group * X_WIDTH, (group + 1) * X_WIDTH)
        x = [acts[step, group, :, :X_WIDTH] for step in range(steps)]
        b = [acts[step, group, :, X_WIDTH : X_WIDTH + N] for step in range(steps)]
        c = [acts[step, group, :, X_WIDTH + N :] for step in range(steps)]
        u = [wide[step, :, span] * x[step] for step in range(steps)]
        first_decay, second_decay, skip = wide[2, :, span], wide[3, :, span], wide[4, :, span]
        held = [jnp.where(live, read[group, step], 0.0) for step in range(steps)]

        def pair_sum(one, two):
            return jnp.sum(one * two, axis=1, keepdims=True)

        later = second_decay * u[0]
        y = [
            first_decay * held[0] + pair_sum(b[0], c[0]) * u[0] + skip * x[0],
            second_decay * first_decay * held[1]
            + pair_sum(b[0], c[1]) * later
            + pair_sum(b[1], c[1]) * u[1]
            + skip * x[1],
        ]
        result = []
        for step in range(steps):
            gated = y[step] * gates[step, :, span]
            scale = lax.rsqrt(jnp.mean(gated * gated, axis=1, keepdims=True) + 1e-05)
            result.append(gated * scale * gain[0:1, span])
        together = jnp.concatenate(result, axis=0).astype(bf16)
        for target in range(out.shape[0]):
            out[target, :ROWS, span] = together
        lines[:, span] = later
        lines[:, channels + group * X_WIDTH : channels + (group + 1) * X_WIDTH] = u[1]
        for step in range(steps):
            start = taps_at + (step * groups + group) * N
            lines[:, start : start + N] = b[step]
    segments = lines.shape[1] // channels
    values = [lines[:, part * channels : (part + 1) * channels] for part in range(segments)]
    high = [value.astype(bf16).astype(f32) for value in values]
    low = [value - near for value, near in zip(values, high)]
    pairs = []
    for row in range(R_PF):
        place = table[plan.row_place + row]
        first = place // plan.cap * ROWS + place % plan.cap * 2 * segments
        pairs += [(first + part, part * R_PF + row) for part in range(2 * segments)]
    matrix = one_hot((out.shape[0] * ROWS, 2 * segments * R_PF), pairs)
    placed = pick(matrix, jnp.concatenate(high + low, axis=0).astype(bf16)).astype(bf16)
    for target in range(out.shape[0]):
        out[target, ROWS:] = placed[target * ROWS : (target + 1) * ROWS]


def run_rows(plan, table, tokens, conv, weight, bias, small, gain, ssm_state, after):
    taps, groups, conv_width = weight.shape
    steps = 2
    heads = ssm_state.shape[1]
    sources = plan.places // plan.cap
    channels = groups * X_WIDTH
    size = -(-packet_places(groups, conv_width)[-1] // channels) * channels
    f32 = jnp.float32
    return pl.pallas_call(
        functools.partial(rows_kernel, plan),
        grid_spec=pltpu.PrefetchScalarGridSpec(
            num_scalar_prefetch=1,
            grid=(1,),
            in_specs=[
                whole(tokens),
                whole(conv),
                whole(weight),
                whole(bias),
                whole(small),
                whole(gain),
                HBM,
            ]
            + [ANY] * len(after),
            out_specs=pl.BlockSpec((sources, 2 * ROWS, channels), lambda i, t: (0, 0, 0)),
            scratch_shapes=[
                pltpu.VMEM((R_PF, heads, P_SIZE, N), f32),
                pltpu.SemaphoreType.DMA((R_PF * PARTS,)),
                pltpu.VMEM((groups, steps, R_PF, X_WIDTH), f32),
                pltpu.VMEM((groups, 2 * steps * R_PF, N), jnp.bfloat16),
                pltpu.VMEM((steps, groups, R_PF, conv_width), f32),
                pltpu.VMEM((5, R_PF, channels), f32),
                pltpu.VMEM((steps, R_PF, channels), f32),
                pltpu.VMEM((R_PF, size), f32),
            ],
        ),
        out_shape=jax.ShapeDtypeStruct((sources, 2 * ROWS, channels), jnp.bfloat16),
        compiler_params=pltpu.CompilerParams(vmem_limit_bytes=VMEM_LARGE),
        name="rows",
    )(table, tokens, conv, weight, bias, small, gain, ssm_state, *after)


def project_kernel(plan, share, table, normed, weight, *refs):
    steps = 2
    targets = plan.rows // share
    own, out, held, total, picked, sems = refs[-6:]
    depth = weight.shape[0]
    piece = depth // BLOCKS

    def copy(block):
        span = pl.ds(block * piece, piece)
        return pltpu.make_async_copy(weight.at[span], held.at[span], sems.at[block])

    for block in range(BLOCKS):
        copy(block).start()

    shape = (steps * plan.rows, steps * plan.rows)
    rows = lax.broadcasted_iota(jnp.int32, shape, 0)
    columns = lax.broadcasted_iota(jnp.int32, shape, 1)

    def add(slot, matrix):
        row = table[plan.slot_row + slot]
        target = slot // share * steps * share + slot % share
        source = (row // R_PF) * steps * R_PF + row % R_PF
        for step in range(steps):
            hit = (rows == target + step * share) & (columns == source + step * R_PF)
            matrix = jnp.where(hit, 1.0, matrix)
        return matrix

    matrix = lax.fori_loop(0, plan.rows, add, jnp.zeros(shape, jnp.float32), unroll=8)
    values = normed[...].reshape(picked.shape)
    picked[...] = pick(matrix.astype(jnp.bfloat16), values).astype(jnp.bfloat16)
    for block in range(BLOCKS):
        copy(block).wait()
        span = slice(block * piece, (block + 1) * piece)
        part = pick(picked[:, span], held[span])
        total[...] = part if block == 0 else total[...] + part
    for target in range(targets):
        part = total[target * steps * share : (target + 1) * steps * share]
        out[target] = part.astype(out.dtype)

        @pl.when(table[plan.head] == target)
        def _():
            own[...] = part


def project(plan, share, table, normed, weight, after):
    depth, columns = weight.shape
    rows = 2 * share
    targets = plan.rows // share
    own = jax.ShapeDtypeStruct((rows, columns), jnp.float32)
    out = jax.ShapeDtypeStruct((targets, rows, columns), jnp.bfloat16)
    return pl.pallas_call(
        functools.partial(project_kernel, plan, share),
        grid_spec=pltpu.PrefetchScalarGridSpec(
            num_scalar_prefetch=1,
            grid=(1,),
            in_specs=[pl.BlockSpec((normed.shape[0], ROWS, depth), lambda i, t: (0, 0, 0)), HBM]
            + [ANY] * len(after),
            out_specs=[whole(own), whole(out)],
            scratch_shapes=[
                pltpu.VMEM(weight.shape, jnp.bfloat16),
                pltpu.VMEM((2 * plan.rows, columns), jnp.float32),
                pltpu.VMEM((2 * plan.rows, depth), jnp.bfloat16),
                pltpu.SemaphoreType.DMA((BLOCKS,)),
            ],
        ),
        out_shape=[own, out],
        compiler_params=pltpu.CompilerParams(vmem_limit_bytes=VMEM_LARGE),
        name="project",
    )(table, normed, weight, *after)


def slots_kernel(plan, decay_at, table, packets, xbc, *refs):
    own, other = refs[-2:]
    f32, bf16 = jnp.float32, jnp.bfloat16
    steps, groups = xbc.shape[:2]
    half = R_PF // 2
    sources, _, channels = packets.shape
    segments = (own.shape[1] - LANES - steps * groups * xbc.shape[3]) // channels
    pairs, order = [], []
    for local in range(R_PF):
        slot = (local + table[plan.parity] * half) % R_PF
        order.append((local, slot))
        place = table[plan.slot_place + slot]
        first = place // plan.cap * ROWS + place % plan.cap * 2 * segments
        pairs += [(part * R_PF + local, first + part) for part in range(2 * segments)]
    matrix = one_hot((2 * segments * R_PF, sources * ROWS), pairs)
    order = one_hot((R_PF, R_PF), order)

    def put(values, start):
        size = values.shape[1]
        own[:, start : start + size] = values[:half].astype(bf16)
        other[:, start : start + size] = values[half:].astype(bf16)

    picked = pick(matrix, packets[...].reshape(sources * ROWS, channels))
    for part in range(segments):
        high = picked[part * R_PF : (part + 1) * R_PF]
        low = picked[(segments + part) * R_PF : (segments + part + 1) * R_PF]
        put(high + low, part * channels)
        if decay_at // channels == part:
            span = slice(decay_at % channels, decay_at % channels + LANES)
            put(low[:, span], segments * channels)
    at = segments * channels + LANES
    for step in range(steps):
        for group in range(groups):
            put(pick(order, xbc[step, group]), at)
            at += xbc.shape[3]


def split_slots(plan, table, packets, xbc, after):
    steps, groups, _, conv_width = xbc.shape
    sources, _, channels = packets.shape
    decay_at, end = packet_places(groups, conv_width)[2:]
    size = -(-end // channels) * channels + LANES + steps * groups * conv_width
    out = jax.ShapeDtypeStruct((R_PF // 2, size), jnp.bfloat16)
    return pl.pallas_call(
        functools.partial(slots_kernel, plan, decay_at),
        grid_spec=pltpu.PrefetchScalarGridSpec(
            num_scalar_prefetch=1,
            grid=(1,),
            in_specs=[
                pl.BlockSpec((sources, ROWS, channels), lambda i, t: (0, 1, 0)),
                whole(xbc),
            ]
            + [ANY] * len(after),
            out_specs=[whole(out)] * 2,
        ),
        out_shape=[out, out],
        compiler_params=pltpu.CompilerParams(vmem_limit_bytes=VMEM_LIMIT),
        name="slots",
    )(table, packets, xbc, *after)


def windows_kernel(plan, groups, conv_width, starts, table, own, got, *refs):
    out = refs[-1]
    parity = table[plan.parity]
    for owner, packet in enumerate((own, got)):
        side = jnp.where(parity == owner, 0, groups)
        for row, start in enumerate(starts):
            for group in range(groups):
                first = start + group * conv_width
                values = packet[:, first : first + conv_width].astype(jnp.float32)
                for slot in range(R_PF // 2):
                    out[0, 0, slot, row, pl.ds(side + group, 1)] = values[slot : slot + 1]


def write_windows(plan, table, own, got, groups, conv_width, starts, after):
    shape = (1, 1, R_PF // 2, len(starts), 2 * groups, conv_width)
    out = jax.ShapeDtypeStruct(shape, jnp.float32)
    return pl.pallas_call(
        functools.partial(windows_kernel, plan, groups, conv_width, starts),
        grid_spec=pltpu.PrefetchScalarGridSpec(
            num_scalar_prefetch=1,
            grid=(1,),
            in_specs=[whole(own), whole(got)] + [ANY] * len(after),
            out_specs=whole(out),
        ),
        out_shape=out,
        compiler_params=pltpu.CompilerParams(vmem_limit_bytes=VMEM_LIMIT),
        name="windows",
    )(table, own, got, *after)


def pack_kernel(plan, places, first, table, state, *refs):
    rows, sems = refs[-2:]
    outputs = refs[-2 - len(places) // plan.cap : -2]
    width = rows.shape[1]

    def copy(index):
        row = table[plan.row_of + places[index]]
        return pltpu.make_async_copy(
            state.at[row, pl.ds(first, width)], rows.at[index], sems.at[index]
        )

    for index in range(len(places)):
        copy(index).start()
    for index in range(len(places)):
        copy(index).wait()
        outputs[index // plan.cap][index % plan.cap] = rows[index].astype(jnp.bfloat16)


def pack_rows(plan, table, ssm_state, shifts, first, width, after):
    cap = plan.cap
    places = [shift * cap + rank for shift in shifts for rank in range(cap)]
    out = jax.ShapeDtypeStruct((cap, width, P_SIZE, N), jnp.bfloat16)
    return pl.pallas_call(
        functools.partial(pack_kernel, plan, places, first),
        grid_spec=pltpu.PrefetchScalarGridSpec(
            num_scalar_prefetch=1,
            grid=(1,),
            in_specs=[HBM] + [ANY] * len(after),
            out_specs=[whole(out)] * len(shifts),
            scratch_shapes=[
                pltpu.VMEM((len(places), width, P_SIZE, N), jnp.float32),
                pltpu.SemaphoreType.DMA((len(places),)),
            ],
        ),
        out_shape=[out] * len(shifts),
        compiler_params=pltpu.CompilerParams(vmem_limit_bytes=VMEM_LIMIT),
        name=f"pack_{first}_{width}",
    )(table, ssm_state, *after)


def route_kernel(plan, sources, table, *refs):
    cap = plan.cap
    arrived, keep, give = refs[:sources], refs[-2], refs[-1]
    half = keep.shape[0]
    for index in range(2 * half):
        target = keep if index < half else give
        place = table[plan.split_place + index]
        for source in range(sources):

            @pl.when(place // cap == source)
            def _():
                target[index % half] = arrived[source][place % cap]


def route_chunk(plan, table, near, far, first, after):
    width = far[0].shape[1]
    half = R_PF // 2
    out = jax.ShapeDtypeStruct((half, width, P_SIZE, N), jnp.bfloat16)
    block = pl.BlockSpec((plan.cap, width, P_SIZE, N), lambda i, rows: (0, first // width - 1, 0, 0))
    return pl.pallas_call(
        functools.partial(route_kernel, plan, len(near) + len(far)),
        grid_spec=pltpu.PrefetchScalarGridSpec(
            num_scalar_prefetch=1,
            grid=(1,),
            in_specs=[block] * len(near) + [whole(one) for one in far] + [ANY] * len(after),
            out_specs=[whole(out)] * 2,
        ),
        out_shape=[out, out],
        compiler_params=pltpu.CompilerParams(vmem_limit_bytes=VMEM_LIMIT),
        name=f"route_{first}_{width}",
    )(table, *near, *far, *after)


def finish_kernel(plan, width, heads, base, table, decay, keep, got, *refs):
    parts, out, done = refs[:8], refs[-2], refs[-1]
    owner = pl.program_id(0)
    slots = keep.shape[0]
    done[...] = jnp.zeros_like(done)

    def fill(source, *pieces):
        first_update, second_update, first_taps, second_taps = [
            piece[...].astype(jnp.float32) for piece in pieces
        ]

        def stack(first, second, slot):
            blank = jnp.zeros((6, first.shape[1]), jnp.float32)
            rows = [first[slot : slot + 1], second[slot : slot + 1], blank]
            return jnp.concatenate(rows, axis=0).astype(jnp.bfloat16)

        for slot in range(slots):
            added = lax.dot_general(
                stack(first_update, second_update, slot),
                stack(first_taps, second_taps, slot),
                (((0,), (0,)), ((), ())),
                preferred_element_type=jnp.float32,
            ).reshape(width, P_SIZE, N)
            for head in range(width):
                factor = decay[(owner * slots + slot) * heads + base + head]
                out[0, 0, slot, head] = (
                    factor * source[slot, head].astype(jnp.float32) + added[head]
                )

    pl.when(owner == 0)(lambda: fill(keep, *parts[:4]))
    pl.when(owner == 1)(lambda: fill(got, *parts[4:]))


def finish_chunk(plan, table, so_far, keep, got, decay, own, other, first, heads):
    slots, width = keep.shape[:2]
    per_half = heads // width
    span = width * P_SIZE
    channels = heads * P_SIZE
    groups = heads // PER_GROUP
    group = first // PER_GROUP
    chunk = first // width
    taps_at = 2 * channels // N
    out_shape = jax.ShapeDtypeStruct((1, 1, slots, 2 * heads, P_SIZE, N), jnp.float32)
    extra = [so_far]

    def part(size, place):
        return pl.BlockSpec((slots, size), lambda o, t, d: (0, place))

    parts = [
        part(span, chunk),
        part(span, channels // span + chunk),
        part(N, taps_at + group),
        part(N, taps_at + groups + group),
    ]
    side = lambda o, t: (o + t[plan.parity]) % 2
    return pl.pallas_call(
        functools.partial(finish_kernel, plan, width, heads, first),
        grid_spec=pltpu.PrefetchScalarGridSpec(
            num_scalar_prefetch=2,
            grid=(2,),
            in_specs=[whole(keep), whole(got)] + parts + parts + [ANY] * len(extra),
            out_specs=[
                pl.BlockSpec(
                    (1, 1, slots, width, P_SIZE, N),
                    lambda o, t, d: (0, 0, 0, side(o, t) * per_half + chunk, 0, 0),
                ),
                pl.BlockSpec((8, 128), lambda o, t, d: (0, 0)),
            ],
        ),
        out_shape=[out_shape, jax.ShapeDtypeStruct((8, 128), jnp.float32)],
        input_output_aliases={12: 0} if so_far.shape == out_shape.shape else {},
        compiler_params=pltpu.CompilerParams(vmem_limit_bytes=VMEM_LIMIT),
        name=f"finish_{first}_{width}",
    )(table, decay, keep, got, *([own] * 4), *([other] * 4), *extra)


def on_device(
    ssm_state,
    conv_state,
    counts,
    request_slot,
    token_xbc,
    token_z,
    token_dt,
    conv_weight,
    conv_bias,
    a_log,
    dt_bias,
    d_skip,
    norm_gain,
    out_weight,
):
    f32 = jnp.float32
    req_count = lax.axis_size("req")
    head_count = lax.axis_size("head")
    plan = Plan(req_count)
    steps = token_xbc.shape[0]
    heads = ssm_state.shape[1]
    groups = conv_state.shape[2]
    conv_width = conv_state.shape[3]
    channels = groups * X_WIDTH

    def shifted(value, axis, shift):
        return lax.ppermute(value, axis, [(i, i ^ shift) for i in range(lax.axis_size(axis))])

    def swap(value):
        return shifted(value, "head", 1)

    def exchange(value, axis):
        return lax.all_to_all(value, axis, split_axis=0, concat_axis=0, tiled=True)

    table = make_plan(plan, request_slot, counts)

    unit = heads // UNITS
    count = len(CHUNKS)
    firsts = [start * unit for start, _ in CHUNKS]
    far, sent = [None] * count, [None] * count
    keeps, gives, gots = [None] * count, [None] * count, [None] * count

    def send(chunk, shifts, after):
        width = CHUNKS[chunk][1] * unit
        packed = pack_rows(plan, table, ssm_state, shifts, firsts[chunk], width, after)
        sent[chunk] = packed[0]
        return [shifted(part, "req", shift) if shift else part for part, shift in zip(packed, shifts)]

    def route(chunk, near, far, after):
        keeps[chunk], gives[chunk] = route_chunk(plan, table, near, far, firsts[chunk], after)
        gots[chunk] = swap(gives[chunk])

    xbc = jnp.swapaxes(token_xbc, 1, 2)
    all_shifts, far_shifts = range(req_count), range(NEAR, req_count)
    far[0] = send(0, all_shifts, [])
    packed_tokens = pack_tokens(plan, table, xbc, token_z, token_dt, [sent[0]])
    tokens = exchange(packed_tokens, "req")
    far[1] = send(1, far_shifts, [packed_tokens])
    route(0, [], far[0], [sent[1], tokens])
    rest = UNITS - CHUNKS[0][1]
    near = pack_rows(
        plan, table, ssm_state, range(NEAR), CHUNKS[0][1] * unit, rest * unit, [sent[1]]
    )
    far[2] = send(2, far_shifts, [gives[0]])
    near = [near[0]] + [shifted(near[shift], "req", shift) for shift in range(1, NEAR)]

    small = jnp.stack([a_log, dt_bias, d_skip]).astype(f32)
    result = run_rows(
        plan,
        table,
        tokens,
        jnp.moveaxis(conv_state, 0, 2),
        conv_weight,
        conv_bias,
        small,
        norm_gain.astype(f32)[None],
        ssm_state,
        [gives[0]],
    )
    route(1, near, far[1], [result, sent[2], gots[0]])
    far[3] = send(3, far_shifts, [gives[1]])
    result = exchange(result, "req")

    share = plan.rows // head_count
    own_sum, sums = project(plan, share, table, result, out_weight, [sent[3]])
    others = exchange(sums, "head").astype(f32)
    is_mine = jnp.arange(head_count) == lax.axis_index("head")
    layer_out = own_sum + jnp.sum(jnp.where(is_mine[:, None, None], 0.0, others), axis=0)
    layer_out = layer_out.astype(jnp.bfloat16).reshape(steps, share, -1)

    own, give = split_slots(plan, table, result, xbc, [sent[3]])
    route(2, near, far[2], [sums, give, gots[1]])
    other = swap(give)
    _, last_at, decay_at, end = packet_places(groups, conv_width)
    low_at = -(-end // channels) * channels
    fresh_at = low_at + LANES
    starts = [last_at] + [fresh_at + step * groups * conv_width for step in range(steps)]
    both = jnp.stack([own, other]).astype(f32)
    decay = both[:, :, decay_at : decay_at + heads] + both[:, :, low_at : low_at + heads]
    decay = decay.reshape(-1)
    route(3, near, far[3], [gots[2]])
    out_conv = write_windows(
        plan, table, own, other, groups, conv_width, starts, [gives[3]]
    )

    out_ssm = gives[-1]
    for chunk in range(count):
        out_ssm, done = finish_chunk(
            plan, table, out_ssm, keeps[chunk], gots[chunk], decay, own, other, firsts[chunk], heads
        )
    return (layer_out, out_ssm, out_conv)


def solution(mesh):
    in_specs = (
        P(("groups", "req"), "head", None, None),
        P(("groups", "req"), None, "head", None),
        P("groups"),
        P("groups"),
        P(None, ("groups", "req"), "head", None),
        P(None, ("groups", "req"), "head"),
        P(None, ("groups", "req"), "head"),
        P(None, "head", None),
        P("head", None),
        P("head"),
        P("head"),
        P("head"),
        P("head"),
        P("head", "req"),
    )
    out_specs = (
        P(None, ("groups", "head"), "req"),
        P(("groups", "req"), "head", None, None, None, None),
        P(("groups", "req"), "head", None, None, None, None),
    )
    return jax.shard_map(
        on_device, mesh=mesh, in_specs=in_specs, out_specs=out_specs, check_vma=False
    )
```

```python
import functools

import jax
import jax.numpy as jnp
from jax import lax
from jax.experimental import pallas as pl
from jax.experimental.pallas import tpu as pltpu
from jax.sharding import PartitionSpec as P

H = 128
P_SIZE = 64
N = 128
G = 8
R_PF = 8
PER_GROUP = H // G
X_WIDTH = PER_GROUP * P_SIZE
CHUNKS = ((0, 2), (4, 4), (2, 2))
UNITS = 8
NEAR = 2
ROWS = 2 * R_PF
PARTS = 4
BLOCKS = 8
LANES = 128
VMEM_LIMIT = 48 * 1024 * 1024
VMEM_LARGE = 48 * 1024 * 1024
ANY = pl.BlockSpec(memory_space=pl.ANY)
HBM = pl.BlockSpec(memory_space=pltpu.HBM)


def split_bf16(value):
    high = value.astype(jnp.bfloat16)
    low = (value - high.astype(jnp.float32)).astype(jnp.bfloat16)
    return high, low


class Plan:
    def __init__(self, req_count):
        self.cap = (R_PF + req_count - 1) // req_count
        self.places = req_count * self.cap
        self.rows = req_count * R_PF
        self.row_of = 0
        self.row_place = self.row_of + self.places
        self.slot_place = self.row_place + R_PF
        self.split_place = self.slot_place + R_PF
        self.live = self.split_place + R_PF
        self.parity = self.live + 1
        self.req = self.parity + 1
        self.head = self.req + 1
        self.slot_row = self.head + 1
        self.size = self.slot_row + self.rows


def plan_kernel(plan, request_slot, counts, out):
    me = lax.axis_index("req")
    parity = lax.axis_index("head") % 2
    half = R_PF // 2
    out[plan.live] = counts[me]
    out[plan.parity] = parity
    out[plan.req] = me
    out[plan.head] = lax.axis_index("head")
    for place in range(plan.places):
        out[plan.row_of + place] = 0

    dests = [request_slot[me * R_PF + row] // R_PF for row in range(R_PF)]
    for row in range(R_PF):
        rank = sum([(dests[row] == dests[other]).astype(jnp.int32) for other in range(row)], 0)
        out[plan.row_place + row] = dests[row] * plan.cap + rank
        out[plan.row_of + (dests[row] ^ me) * plan.cap + rank] = row

    @pl.loop(0, plan.rows // R_PF)
    def _(group):
        seen = jnp.int32(0)
        for row in range(R_PF):
            slot = request_slot[group * R_PF + row]
            out[plan.slot_row + slot] = group * R_PF + row
            here = slot // R_PF == me
            local = slot % R_PF

            @pl.when(here)
            def _():
                out[plan.slot_place + local] = group * plan.cap + seen
                out[plan.split_place + (local + parity * half) % R_PF] = (
                    group ^ me
                ) * plan.cap + seen

            seen = seen + here.astype(jnp.int32)


def make_plan(plan, request_slot, counts):
    smem = pl.BlockSpec(memory_space=pltpu.SMEM)
    return pl.pallas_call(
        functools.partial(plan_kernel, plan),
        in_specs=[smem, smem],
        out_specs=smem,
        out_shape=jax.ShapeDtypeStruct((plan.size,), jnp.int32),
        compiler_params=pltpu.CompilerParams(vmem_limit_bytes=VMEM_LIMIT),
        name="plan",
    )(request_slot, counts)


def one_hot(shape, pairs):
    rows = lax.broadcasted_iota(jnp.int32, shape, 0)
    columns = lax.broadcasted_iota(jnp.int32, shape, 1)
    total = jnp.zeros(shape, jnp.float32)
    for row, column in pairs:
        total = jnp.where((rows == row) & (columns == column), 1.0, total)
    return total.astype(jnp.bfloat16)


def pick(matrix, values):
    return jnp.dot(matrix, values, preferred_element_type=jnp.float32)


def tokens_kernel(plan, table, xbc, z, dt, *refs):
    out = refs[-1]
    steps, groups = xbc.shape[:2]
    matrix = one_hot(
        (plan.places, R_PF), [(table[plan.slot_place + slot], slot) for slot in range(R_PF)]
    )

    def put(values, start):
        picked = pick(matrix, values)
        size = values.shape[1]
        for source in range(plan.places // plan.cap):
            rows = picked[source * plan.cap : (source + 1) * plan.cap]
            out[source, :, start : start + size] = rows.astype(jnp.bfloat16)

    at = 0
    for step in range(steps):
        for group in range(groups):
            put(xbc[step, group], at)
            at += xbc.shape[3]
        put(z[step], at)
        at += z.shape[2]
        put(dt[step], at)
        at += LANES


def pack_tokens(plan, table, xbc, z, dt, after):
    steps, groups = xbc.shape[:2]
    size = steps * (groups * xbc.shape[3] + z.shape[2] + LANES)
    return pl.pallas_call(
        functools.partial(tokens_kernel, plan),
        grid_spec=pltpu.PrefetchScalarGridSpec(
            num_scalar_prefetch=1,
            grid=(1,),
            in_specs=[whole(xbc), whole(z), whole(dt)] + [ANY] * len(after),
            out_specs=pl.BlockSpec((plan.places // plan.cap, plan.cap, size), lambda i, t: (0, 0, 0)),
        ),
        out_shape=jax.ShapeDtypeStruct((plan.places // plan.cap, plan.cap, size), jnp.bfloat16),
        compiler_params=pltpu.CompilerParams(vmem_limit_bytes=VMEM_LIMIT),
        name="tokens",
    )(table, xbc, z, dt, *after)


def whole(array):
    return pl.BlockSpec(array.shape, lambda *_: (0,) * array.ndim)


def silu(value):
    return value / (1.0 + jnp.exp(-value))


def packet_places(groups, conv_width):
    taps_at = 2 * groups * X_WIDTH
    last_at = taps_at + 2 * groups * N
    decay_at = last_at + groups * conv_width
    return taps_at, last_at, decay_at, decay_at + LANES


def rows_kernel(plan, table, tokens, conv, weight, bias, small, gain, state, *refs):
    out, states, sems, read, read_taps, acts, wide, gates, lines = refs[-9:]
    steps = 2
    taps, groups, conv_width = weight.shape
    heads = state.shape[1]
    channels = groups * X_WIDTH
    row_ids = lax.broadcasted_iota(jnp.int32, (R_PF, 1), 0)
    live = row_ids < table[plan.live]
    f32, bf16 = jnp.float32, jnp.bfloat16
    taps_at, last_at, decay_at, _ = packet_places(groups, conv_width)

    share = heads // PARTS

    def copy(row, part):
        span = pl.ds(part * share, share)
        return pltpu.make_async_copy(
            state.at[row, span], states.at[row, span], sems.at[row * PARTS + part]
        )

    for row in range(R_PF):
        for part in range(PARTS):
            copy(row, part).start()

    matrix = one_hot(
        (R_PF, plan.places), [(row, table[plan.row_place + row]) for row in range(R_PF)]
    )
    stride = tokens.shape[2] // steps

    def rows_of(start, size):
        parts = [tokens[source, :, start : start + size] for source in range(tokens.shape[0])]
        parts = jnp.concatenate([part.astype(f32) for part in parts], axis=0)
        return pick(matrix, parts.astype(bf16))

    for group in range(groups):
        window = [
            jnp.where(live, conv[tap, group], 0.0) for tap in range(taps - 1)
        ] + [
            rows_of(step * stride + group * conv_width, conv_width) for step in range(steps)
        ]
        kernel = [weight[tap].astype(f32)[group : group + 1] for tap in range(taps)]
        offset = bias[...].astype(f32)[group : group + 1]
        parts = []
        for step in range(steps):
            total = sum(window[step + tap] * kernel[tap] for tap in range(taps)) + offset
            act = silu(total)
            acts[step, group] = act
            parts.append(act[:, X_WIDTH + N :])
        high = [part.astype(bf16).astype(f32) for part in parts]
        low = [part - near for part, near in zip(parts, high)]
        read_taps[group] = jnp.concatenate(high + low, axis=0).astype(bf16)
        start = last_at + group * conv_width
        lines[:, start : start + conv_width] = window[taps - 2]

    dts, decays = [], []
    rate = jnp.exp(small[0:1, :heads])
    for step in range(steps):
        base = step * stride + groups * conv_width
        gates[step] = silu(rows_of(base, channels))
        raw = rows_of(base + channels, LANES)[:, :heads] + small[1:2, :heads]
        dts.append(jnp.maximum(raw, 0.0) + jnp.log1p(jnp.exp(-jnp.abs(raw))))
        decays.append(jnp.exp(-dts[-1] * rate))
    lines[:, decay_at : decay_at + LANES] = jnp.concatenate(
        [jnp.where(live, decays[0] * decays[1], 0.0), jnp.zeros((R_PF, LANES - heads), f32)],
        axis=1,
    )
    skip = jnp.broadcast_to(small[2:3, :heads], (R_PF, heads))
    narrow = jnp.concatenate(dts + decays + [skip], axis=0)
    high = narrow.astype(bf16).astype(f32)
    middle = (narrow - high).astype(bf16).astype(f32)
    narrow = jnp.concatenate([high, middle, narrow - high - middle], axis=1).astype(bf16)
    head_ids = lax.broadcasted_iota(jnp.int32, (3 * heads, channels), 0) % heads
    channel_ids = lax.broadcasted_iota(jnp.int32, (3 * heads, channels), 1) // P_SIZE
    spread = pick(narrow, (head_ids == channel_ids).astype(bf16))
    for part in range(5):
        wide[part] = spread[part * R_PF : (part + 1) * R_PF]

    @pl.loop(0, R_PF)
    def _(index):
        for part in range(PARTS):
            copy(index, part).wait()
            size = share * P_SIZE
            group, start = part * size // X_WIDTH, part * size % X_WIDTH
            rows = states[index, part * share : (part + 1) * share].reshape(size, N)
            state_high, state_low = split_bf16(rows)
            dims = (((1,), (1,)), ((), ()))
            total = lax.dot_general(read_taps[group], state_high, dims, preferred_element_type=f32)
            rest = lax.dot_general(
                read_taps[group, : steps * R_PF], state_low, dims, preferred_element_type=f32
            )
            total = total[: steps * R_PF] + total[steps * R_PF :] + rest
            for step in range(steps):
                now = total[step * R_PF : (step + 1) * R_PF]
                span = slice(start, start + size)
                read[group, step, :, span] = jnp.where(
                    row_ids == index, now, read[group, step, :, span]
                )

    for group in range(groups):
        span = slice(group * X_WIDTH, (group + 1) * X_WIDTH)
        x = [acts[step, group, :, :X_WIDTH] for step in range(steps)]
        b = [acts[step, group, :, X_WIDTH : X_WIDTH + N] for step in range(steps)]
        c = [acts[step, group, :, X_WIDTH + N :] for step in range(steps)]
        u = [wide[step, :, span] * x[step] for step in range(steps)]
        first_decay, second_decay, skip = wide[2, :, span], wide[3, :, span], wide[4, :, span]
        held = [jnp.where(live, read[group, step], 0.0) for step in range(steps)]

        def pair_sum(one, two):
            return jnp.sum(one * two, axis=1, keepdims=True)

        later = second_decay * u[0]
        y = [
            first_decay * held[0] + pair_sum(b[0], c[0]) * u[0] + skip * x[0],
            second_decay * first_decay * held[1]
            + pair_sum(b[0], c[1]) * later
            + pair_sum(b[1], c[1]) * u[1]
            + skip * x[1],
        ]
        result = []
        for step in range(steps):
            gated = y[step] * gates[step, :, span]
            scale = lax.rsqrt(jnp.mean(gated * gated, axis=1, keepdims=True) + 1e-05)
            result.append(gated * scale * gain[0:1, span])
        together = jnp.concatenate(result, axis=0).astype(bf16)
        for target in range(out.shape[0]):
            out[target, :ROWS, span] = together
        lines[:, span] = later
        lines[:, channels + group * X_WIDTH : channels + (group + 1) * X_WIDTH] = u[1]
        for step in range(steps):
            start = taps_at + (step * groups + group) * N
            lines[:, start : start + N] = b[step]
    segments = lines.shape[1] // channels
    values = [lines[:, part * channels : (part + 1) * channels] for part in range(segments)]
    high = [value.astype(bf16).astype(f32) for value in values]
    low = [value - near for value, near in zip(values, high)]
    pairs = []
    for row in range(R_PF):
        place = table[plan.row_place + row]
        first = place // plan.cap * ROWS + place % plan.cap * 2 * segments
        pairs += [(first + part, part * R_PF + row) for part in range(2 * segments)]
    matrix = one_hot((out.shape[0] * ROWS, 2 * segments * R_PF), pairs)
    placed = pick(matrix, jnp.concatenate(high + low, axis=0).astype(bf16)).astype(bf16)
    for target in range(out.shape[0]):
        out[target, ROWS:] = placed[target * ROWS : (target + 1) * ROWS]


def run_rows(plan, table, tokens, conv, weight, bias, small, gain, ssm_state, after):
    taps, groups, conv_width = weight.shape
    steps = 2
    heads = ssm_state.shape[1]
    sources = plan.places // plan.cap
    channels = groups * X_WIDTH
    size = -(-packet_places(groups, conv_width)[-1] // channels) * channels
    f32 = jnp.float32
    return pl.pallas_call(
        functools.partial(rows_kernel, plan),
        grid_spec=pltpu.PrefetchScalarGridSpec(
            num_scalar_prefetch=1,
            grid=(1,),
            in_specs=[
                whole(tokens),
                whole(conv),
                whole(weight),
                whole(bias),
                whole(small),
                whole(gain),
                HBM,
            ]
            + [ANY] * len(after),
            out_specs=pl.BlockSpec((sources, 2 * ROWS, channels), lambda i, t: (0, 0, 0)),
            scratch_shapes=[
                pltpu.VMEM((R_PF, heads, P_SIZE, N), f32),
                pltpu.SemaphoreType.DMA((R_PF * PARTS,)),
                pltpu.VMEM((groups, steps, R_PF, X_WIDTH), f32),
                pltpu.VMEM((groups, 2 * steps * R_PF, N), jnp.bfloat16),
                pltpu.VMEM((steps, groups, R_PF, conv_width), f32),
                pltpu.VMEM((5, R_PF, channels), f32),
                pltpu.VMEM((steps, R_PF, channels), f32),
                pltpu.VMEM((R_PF, size), f32),
            ],
        ),
        out_shape=jax.ShapeDtypeStruct((sources, 2 * ROWS, channels), jnp.bfloat16),
        compiler_params=pltpu.CompilerParams(vmem_limit_bytes=VMEM_LARGE),
        name="rows",
    )(table, tokens, conv, weight, bias, small, gain, ssm_state, *after)


def project_kernel(plan, share, table, normed, weight, *refs):
    steps = 2
    targets = plan.rows // share
    own, out, held, total, picked, sems = refs[-6:]
    depth = weight.shape[0]
    piece = depth // BLOCKS

    def copy(block):
        span = pl.ds(block * piece, piece)
        return pltpu.make_async_copy(weight.at[span], held.at[span], sems.at[block])

    for block in range(BLOCKS):
        copy(block).start()

    shape = (steps * plan.rows, steps * plan.rows)
    rows = lax.broadcasted_iota(jnp.int32, shape, 0)
    columns = lax.broadcasted_iota(jnp.int32, shape, 1)

    def add(slot, matrix):
        row = table[plan.slot_row + slot]
        target = slot // share * steps * share + slot % share
        source = (row // R_PF) * steps * R_PF + row % R_PF
        for step in range(steps):
            hit = (rows == target + step * share) & (columns == source + step * R_PF)
            matrix = jnp.where(hit, 1.0, matrix)
        return matrix

    matrix = lax.fori_loop(0, plan.rows, add, jnp.zeros(shape, jnp.float32), unroll=8)
    values = normed[...].reshape(picked.shape)
    picked[...] = pick(matrix.astype(jnp.bfloat16), values).astype(jnp.bfloat16)
    for block in range(BLOCKS):
        copy(block).wait()
        span = slice(block * piece, (block + 1) * piece)
        part = pick(picked[:, span], held[span])
        total[...] = part if block == 0 else total[...] + part
    for target in range(targets):
        part = total[target * steps * share : (target + 1) * steps * share]
        out[target] = part.astype(out.dtype)

        @pl.when(table[plan.head] == target)
        def _():
            own[...] = part


def project(plan, share, table, normed, weight, after):
    depth, columns = weight.shape
    rows = 2 * share
    targets = plan.rows // share
    own = jax.ShapeDtypeStruct((rows, columns), jnp.float32)
    out = jax.ShapeDtypeStruct((targets, rows, columns), jnp.bfloat16)
    return pl.pallas_call(
        functools.partial(project_kernel, plan, share),
        grid_spec=pltpu.PrefetchScalarGridSpec(
            num_scalar_prefetch=1,
            grid=(1,),
            in_specs=[pl.BlockSpec((normed.shape[0], ROWS, depth), lambda i, t: (0, 0, 0)), HBM]
            + [ANY] * len(after),
            out_specs=[whole(own), whole(out)],
            scratch_shapes=[
                pltpu.VMEM(weight.shape, jnp.bfloat16),
                pltpu.VMEM((2 * plan.rows, columns), jnp.float32),
                pltpu.VMEM((2 * plan.rows, depth), jnp.bfloat16),
                pltpu.SemaphoreType.DMA((BLOCKS,)),
            ],
        ),
        out_shape=[own, out],
        compiler_params=pltpu.CompilerParams(vmem_limit_bytes=VMEM_LARGE),
        name="project",
    )(table, normed, weight, *after)


def slots_kernel(plan, decay_at, table, packets, xbc, *refs):
    own, other = refs[-2:]
    f32, bf16 = jnp.float32, jnp.bfloat16
    steps, groups = xbc.shape[:2]
    half = R_PF // 2
    sources, _, channels = packets.shape
    segments = (own.shape[1] - LANES - steps * groups * xbc.shape[3]) // channels
    pairs, order = [], []
    for local in range(R_PF):
        slot = (local + table[plan.parity] * half) % R_PF
        order.append((local, slot))
        place = table[plan.slot_place + slot]
        first = place // plan.cap * ROWS + place % plan.cap * 2 * segments
        pairs += [(part * R_PF + local, first + part) for part in range(2 * segments)]
    matrix = one_hot((2 * segments * R_PF, sources * ROWS), pairs)
    order = one_hot((R_PF, R_PF), order)

    def put(values, start):
        size = values.shape[1]
        own[:, start : start + size] = values[:half].astype(bf16)
        other[:, start : start + size] = values[half:].astype(bf16)

    picked = pick(matrix, packets[...].reshape(sources * ROWS, channels))
    for part in range(segments):
        high = picked[part * R_PF : (part + 1) * R_PF]
        low = picked[(segments + part) * R_PF : (segments + part + 1) * R_PF]
        put(high + low, part * channels)
        if decay_at // channels == part:
            span = slice(decay_at % channels, decay_at % channels + LANES)
            put(low[:, span], segments * channels)
    at = segments * channels + LANES
    for step in range(steps):
        for group in range(groups):
            put(pick(order, xbc[step, group]), at)
            at += xbc.shape[3]


def split_slots(plan, table, packets, xbc, after):
    steps, groups, _, conv_width = xbc.shape
    sources, _, channels = packets.shape
    decay_at, end = packet_places(groups, conv_width)[2:]
    size = -(-end // channels) * channels + LANES + steps * groups * conv_width
    out = jax.ShapeDtypeStruct((R_PF // 2, size), jnp.bfloat16)
    return pl.pallas_call(
        functools.partial(slots_kernel, plan, decay_at),
        grid_spec=pltpu.PrefetchScalarGridSpec(
            num_scalar_prefetch=1,
            grid=(1,),
            in_specs=[
                pl.BlockSpec((sources, ROWS, channels), lambda i, t: (0, 1, 0)),
                whole(xbc),
            ]
            + [ANY] * len(after),
            out_specs=[whole(out)] * 2,
        ),
        out_shape=[out, out],
        compiler_params=pltpu.CompilerParams(vmem_limit_bytes=VMEM_LIMIT),
        name="slots",
    )(table, packets, xbc, *after)


def windows_kernel(plan, groups, conv_width, starts, table, own, got, *refs):
    out = refs[-1]
    parity = table[plan.parity]
    for owner, packet in enumerate((own, got)):
        side = jnp.where(parity == owner, 0, groups)
        for row, start in enumerate(starts):
            for group in range(groups):
                first = start + group * conv_width
                values = packet[:, first : first + conv_width].astype(jnp.float32)
                for slot in range(R_PF // 2):
                    out[0, 0, slot, row, pl.ds(side + group, 1)] = values[slot : slot + 1]


def write_windows(plan, table, own, got, groups, conv_width, starts, after):
    shape = (1, 1, R_PF // 2, len(starts), 2 * groups, conv_width)
    out = jax.ShapeDtypeStruct(shape, jnp.float32)
    return pl.pallas_call(
        functools.partial(windows_kernel, plan, groups, conv_width, starts),
        grid_spec=pltpu.PrefetchScalarGridSpec(
            num_scalar_prefetch=1,
            grid=(1,),
            in_specs=[whole(own), whole(got)] + [ANY] * len(after),
            out_specs=whole(out),
        ),
        out_shape=out,
        compiler_params=pltpu.CompilerParams(vmem_limit_bytes=VMEM_LIMIT),
        name="windows",
    )(table, own, got, *after)


def pack_kernel(plan, places, first, table, state, *refs):
    rows, sems = refs[-2:]
    outputs = refs[-2 - len(places) // plan.cap : -2]
    width = rows.shape[1]

    def copy(index):
        row = table[plan.row_of + places[index]]
        return pltpu.make_async_copy(
            state.at[row, pl.ds(first, width)], rows.at[index], sems.at[index]
        )

    for index in range(len(places)):
        copy(index).start()
    for index in range(len(places)):
        copy(index).wait()
        outputs[index // plan.cap][index % plan.cap] = rows[index].astype(jnp.bfloat16)


def pack_rows(plan, table, ssm_state, shifts, first, width, after):
    cap = plan.cap
    places = [shift * cap + rank for shift in shifts for rank in range(cap)]
    out = jax.ShapeDtypeStruct((cap, width, P_SIZE, N), jnp.bfloat16)
    return pl.pallas_call(
        functools.partial(pack_kernel, plan, places, first),
        grid_spec=pltpu.PrefetchScalarGridSpec(
            num_scalar_prefetch=1,
            grid=(1,),
            in_specs=[HBM] + [ANY] * len(after),
            out_specs=[whole(out)] * len(shifts),
            scratch_shapes=[
                pltpu.VMEM((len(places), width, P_SIZE, N), jnp.float32),
                pltpu.SemaphoreType.DMA((len(places),)),
            ],
        ),
        out_shape=[out] * len(shifts),
        compiler_params=pltpu.CompilerParams(vmem_limit_bytes=VMEM_LIMIT),
        name=f"pack_{first}_{width}",
    )(table, ssm_state, *after)


def route_kernel(plan, sources, nears, offset, table, *refs):
    cap = plan.cap
    arrived, keep, give = refs[:sources], refs[-2], refs[-1]
    half = keep.shape[0]
    for index in range(2 * half):
        target = keep if index < half else give
        place = table[plan.split_place + index]
        for source in range(sources):

            @pl.when(place // cap == source)
            def _():
                if source < nears:
                    span = pl.ds(offset, target.shape[1])
                    target[index % half] = arrived[source][place % cap, span]
                else:
                    target[index % half] = arrived[source][place % cap]


def route_chunk(plan, table, near, far, first, offset, after):
    width = far[0].shape[1]
    half = R_PF // 2
    out = jax.ShapeDtypeStruct((half, width, P_SIZE, N), jnp.bfloat16)
    return pl.pallas_call(
        functools.partial(route_kernel, plan, len(near) + len(far), len(near), offset),
        grid_spec=pltpu.PrefetchScalarGridSpec(
            num_scalar_prefetch=1,
            grid=(1,),
            in_specs=[whole(one) for one in [*near, *far]] + [ANY] * len(after),
            out_specs=[whole(out)] * 2,
        ),
        out_shape=[out, out],
        compiler_params=pltpu.CompilerParams(vmem_limit_bytes=VMEM_LIMIT),
        name=f"route_{first}_{width}",
    )(table, *near, *far, *after)


def finish_kernel(plan, width, heads, base, table, decay, keep, got, *refs):
    parts, out, done = refs[:8], refs[-2], refs[-1]
    owner = pl.program_id(0)
    slots = keep.shape[0]
    done[...] = jnp.zeros_like(done)

    def fill(source, *pieces):
        first_update, second_update, first_taps, second_taps = [
            piece[...].astype(jnp.float32) for piece in pieces
        ]

        def stack(first, second, slot):
            blank = jnp.zeros((6, first.shape[1]), jnp.float32)
            rows = [first[slot : slot + 1], second[slot : slot + 1], blank]
            return jnp.concatenate(rows, axis=0).astype(jnp.bfloat16)

        for slot in range(slots):
            added = lax.dot_general(
                stack(first_update, second_update, slot),
                stack(first_taps, second_taps, slot),
                (((0,), (0,)), ((), ())),
                preferred_element_type=jnp.float32,
            ).reshape(width, P_SIZE, N)
            for head in range(width):
                factor = decay[(owner * slots + slot) * heads + base + head]
                out[0, 0, slot, head] = (
                    factor * source[slot, head].astype(jnp.float32) + added[head]
                )

    pl.when(owner == 0)(lambda: fill(keep, *parts[:4]))
    pl.when(owner == 1)(lambda: fill(got, *parts[4:]))


def finish_chunk(plan, table, so_far, keep, got, decay, own, other, first, heads):
    slots, width = keep.shape[:2]
    per_half = heads // width
    span = width * P_SIZE
    channels = heads * P_SIZE
    groups = heads // PER_GROUP
    group = first // PER_GROUP
    chunk = first // width
    taps_at = 2 * channels // N
    out_shape = jax.ShapeDtypeStruct((1, 1, slots, 2 * heads, P_SIZE, N), jnp.float32)
    extra = [so_far]

    def part(size, place):
        return pl.BlockSpec((slots, size), lambda o, t, d: (0, place))

    parts = [
        part(span, chunk),
        part(span, channels // span + chunk),
        part(N, taps_at + group),
        part(N, taps_at + groups + group),
    ]
    side = lambda o, t: (o + t[plan.parity]) % 2
    return pl.pallas_call(
        functools.partial(finish_kernel, plan, width, heads, first),
        grid_spec=pltpu.PrefetchScalarGridSpec(
            num_scalar_prefetch=2,
            grid=(2,),
            in_specs=[whole(keep), whole(got)] + parts + parts + [ANY] * len(extra),
            out_specs=[
                pl.BlockSpec(
                    (1, 1, slots, width, P_SIZE, N),
                    lambda o, t, d: (0, 0, 0, side(o, t) * per_half + chunk, 0, 0),
                ),
                pl.BlockSpec((8, 128), lambda o, t, d: (0, 0)),
            ],
        ),
        out_shape=[out_shape, jax.ShapeDtypeStruct((8, 128), jnp.float32)],
        input_output_aliases={12: 0} if so_far.shape == out_shape.shape else {},
        compiler_params=pltpu.CompilerParams(vmem_limit_bytes=VMEM_LIMIT),
        name=f"finish_{first}_{width}",
    )(table, decay, keep, got, *([own] * 4), *([other] * 4), *extra)


def on_device(
    ssm_state,
    conv_state,
    counts,
    request_slot,
    token_xbc,
    token_z,
    token_dt,
    conv_weight,
    conv_bias,
    a_log,
    dt_bias,
    d_skip,
    norm_gain,
    out_weight,
):
    f32 = jnp.float32
    req_count = lax.axis_size("req")
    head_count = lax.axis_size("head")
    plan = Plan(req_count)
    steps = token_xbc.shape[0]
    heads = ssm_state.shape[1]
    groups = conv_state.shape[2]
    conv_width = conv_state.shape[3]
    channels = groups * X_WIDTH

    def shifted(value, axis, shift):
        return lax.ppermute(value, axis, [(i, i ^ shift) for i in range(lax.axis_size(axis))])

    def swap(value):
        return shifted(value, "head", 1)

    def exchange(value, axis):
        return lax.all_to_all(value, axis, split_axis=0, concat_axis=0, tiled=True)

    table = make_plan(plan, request_slot, counts)

    unit = heads // UNITS
    count = len(CHUNKS)
    firsts = [start * unit for start, _ in CHUNKS]
    far, sent = [None] * count, [None] * count
    keeps, gives, gots = [None] * count, [None] * count, [None] * count

    def send(chunk, shifts, after):
        width = CHUNKS[chunk][1] * unit
        packed = pack_rows(plan, table, ssm_state, shifts, firsts[chunk], width, after)
        sent[chunk] = packed[0]
        return [shifted(part, "req", shift) if shift else part for part, shift in zip(packed, shifts)]

    def route(chunk, near, far, after):
        keeps[chunk], gives[chunk] = route_chunk(
            plan, table, near, far, firsts[chunk], firsts[chunk] - CHUNKS[0][1] * unit, after
        )
        gots[chunk] = swap(gives[chunk])

    xbc = jnp.swapaxes(token_xbc, 1, 2)
    all_shifts, far_shifts = range(req_count), range(NEAR, req_count)
    far[0] = send(0, all_shifts, [])
    packed_tokens = pack_tokens(plan, table, xbc, token_z, token_dt, [sent[0]])
    tokens = exchange(packed_tokens, "req")
    far[1] = send(1, far_shifts, [packed_tokens])
    route(0, [], far[0], [sent[1], tokens])
    rest = UNITS - CHUNKS[0][1]
    near = pack_rows(
        plan, table, ssm_state, range(NEAR), CHUNKS[0][1] * unit, rest * unit, [sent[1]]
    )
    far[2] = send(2, far_shifts, [gives[0]])
    near = [near[0]] + [shifted(near[shift], "req", shift) for shift in range(1, NEAR)]

    small = jnp.stack([a_log, dt_bias, d_skip]).astype(f32)
    result = run_rows(
        plan,
        table,
        tokens,
        jnp.moveaxis(conv_state, 0, 2),
        conv_weight,
        conv_bias,
        small,
        norm_gain.astype(f32)[None],
        ssm_state,
        [gives[0]],
    )
    route(1, near, far[1], [sent[2], gots[0], result])
    result = exchange(result, "req")
    share = plan.rows // head_count
    own_sum, sums = project(plan, share, table, result, out_weight, [gives[1]])
    others = exchange(sums, "head").astype(f32)
    is_mine = jnp.arange(head_count) == lax.axis_index("head")
    layer_out = own_sum + jnp.sum(jnp.where(is_mine[:, None, None], 0.0, others), axis=0)
    layer_out = layer_out.astype(jnp.bfloat16).reshape(steps, share, -1)

    own, give = split_slots(plan, table, result, xbc, far[2])
    other = swap(give)
    route(2, near, far[2], [sums, other, gots[1]])
    _, last_at, decay_at, end = packet_places(groups, conv_width)
    low_at = -(-end // channels) * channels
    fresh_at = low_at + LANES
    starts = [last_at] + [fresh_at + step * groups * conv_width for step in range(steps)]
    both = jnp.stack([own, other]).astype(f32)
    decay = both[:, :, decay_at : decay_at + heads] + both[:, :, low_at : low_at + heads]
    decay = decay.reshape(-1)
    out_conv = write_windows(
        plan, table, own, other, groups, conv_width, starts, [gives[2]]
    )

    out_ssm = gives[-1]
    for chunk in range(count):
        out_ssm, done = finish_chunk(
            plan, table, out_ssm, keeps[chunk], gots[chunk], decay, own, other, firsts[chunk], heads
        )
    return (layer_out, out_ssm, out_conv)


def solution(mesh):
    in_specs = (
        P(("groups", "req"), "head", None, None),
        P(("groups", "req"), None, "head", None),
        P("groups"),
        P("groups"),
        P(None, ("groups", "req"), "head", None),
        P(None, ("groups", "req"), "head"),
        P(None, ("groups", "req"), "head"),
        P(None, "head", None),
        P("head", None),
        P("head"),
        P("head"),
        P("head"),
        P("head"),
        P("head", "req"),
    )
    out_specs = (
        P(None, ("groups", "head"), "req"),
        P(("groups", "req"), "head", None, None, None, None),
        P(("groups", "req"), "head", None, None, None, None),
    )
    return jax.shard_map(
        on_device, mesh=mesh, in_specs=in_specs, out_specs=out_specs, check_vma=False
    )
```

```python
import functools

import jax
import jax.numpy as jnp
from jax import lax
from jax.experimental import pallas as pl
from jax.experimental.pallas import tpu as pltpu
from jax.sharding import PartitionSpec as P

H = 128
P_SIZE = 64
N = 128
G = 8
R_PF = 8
PER_GROUP = H // G
X_WIDTH = PER_GROUP * P_SIZE
CHUNKS = ((0, 2), (4, 4), (2, 2))
UNITS = 8
NEAR = 2
ROWS = 2 * R_PF
PARTS = 4
BLOCKS = 8
LANES = 128
VMEM_LIMIT = 53 * 1024 * 1024
VMEM_LARGE = 53 * 1024 * 1024
ANY = pl.BlockSpec(memory_space=pl.ANY)
HBM = pl.BlockSpec(memory_space=pltpu.HBM)


def split_bf16(value):
    high = value.astype(jnp.bfloat16)
    low = (value - high.astype(jnp.float32)).astype(jnp.bfloat16)
    return high, low


class Plan:
    def __init__(self, req_count):
        self.cap = (R_PF + req_count - 1) // req_count
        self.places = req_count * self.cap
        self.rows = req_count * R_PF
        self.row_of = 0
        self.row_place = self.row_of + self.places
        self.slot_place = self.row_place + R_PF
        self.split_place = self.slot_place + R_PF
        self.live = self.split_place + R_PF
        self.parity = self.live + 1
        self.req = self.parity + 1
        self.head = self.req + 1
        self.slot_row = self.head + 1
        self.size = self.slot_row + self.rows


def plan_kernel(plan, request_slot, counts, out):
    me = lax.axis_index("req")
    parity = lax.axis_index("head") % 2
    half = R_PF // 2
    out[plan.live] = counts[me]
    out[plan.parity] = parity
    out[plan.req] = me
    out[plan.head] = lax.axis_index("head")
    for place in range(plan.places):
        out[plan.row_of + place] = 0

    dests = [request_slot[me * R_PF + row] // R_PF for row in range(R_PF)]
    for row in range(R_PF):
        rank = sum([(dests[row] == dests[other]).astype(jnp.int32) for other in range(row)], 0)
        out[plan.row_place + row] = dests[row] * plan.cap + rank
        out[plan.row_of + (dests[row] ^ me) * plan.cap + rank] = row

    @pl.loop(0, plan.rows // R_PF)
    def _(group):
        seen = jnp.int32(0)
        for row in range(R_PF):
            slot = request_slot[group * R_PF + row]
            out[plan.slot_row + slot] = group * R_PF + row
            here = slot // R_PF == me
            local = slot % R_PF

            @pl.when(here)
            def _():
                out[plan.slot_place + local] = group * plan.cap + seen
                out[plan.split_place + (local + parity * half) % R_PF] = (
                    group ^ me
                ) * plan.cap + seen

            seen = seen + here.astype(jnp.int32)


def make_plan(plan, request_slot, counts):
    smem = pl.BlockSpec(memory_space=pltpu.SMEM)
    return pl.pallas_call(
        functools.partial(plan_kernel, plan),
        in_specs=[smem, smem],
        out_specs=smem,
        out_shape=jax.ShapeDtypeStruct((plan.size,), jnp.int32),
        compiler_params=pltpu.CompilerParams(vmem_limit_bytes=VMEM_LIMIT),
        name="plan",
    )(request_slot, counts)


def one_hot(shape, pairs):
    rows = lax.broadcasted_iota(jnp.int32, shape, 0)
    columns = lax.broadcasted_iota(jnp.int32, shape, 1)
    total = jnp.zeros(shape, jnp.float32)
    for row, column in pairs:
        total = jnp.where((rows == row) & (columns == column), 1.0, total)
    return total.astype(jnp.bfloat16)


def pick(matrix, values):
    return jnp.dot(matrix, values, preferred_element_type=jnp.float32)


def tokens_kernel(plan, table, xbc, z, dt, *refs):
    out = refs[-1]
    steps, groups = xbc.shape[:2]
    matrix = one_hot(
        (plan.places, R_PF), [(table[plan.slot_place + slot], slot) for slot in range(R_PF)]
    )

    def put(values, start):
        picked = pick(matrix, values)
        size = values.shape[1]
        for source in range(plan.places // plan.cap):
            rows = picked[source * plan.cap : (source + 1) * plan.cap]
            out[source, :, start : start + size] = rows.astype(jnp.bfloat16)

    at = 0
    for step in range(steps):
        for group in range(groups):
            put(xbc[step, group], at)
            at += xbc.shape[3]
        put(z[step], at)
        at += z.shape[2]
        put(dt[step], at)
        at += LANES


def pack_tokens(plan, table, xbc, z, dt, after):
    steps, groups = xbc.shape[:2]
    size = steps * (groups * xbc.shape[3] + z.shape[2] + LANES)
    return pl.pallas_call(
        functools.partial(tokens_kernel, plan),
        grid_spec=pltpu.PrefetchScalarGridSpec(
            num_scalar_prefetch=1,
            grid=(1,),
            in_specs=[whole(xbc), whole(z), whole(dt)] + [ANY] * len(after),
            out_specs=pl.BlockSpec((plan.places // plan.cap, plan.cap, size), lambda i, t: (0, 0, 0)),
        ),
        out_shape=jax.ShapeDtypeStruct((plan.places // plan.cap, plan.cap, size), jnp.bfloat16),
        compiler_params=pltpu.CompilerParams(vmem_limit_bytes=VMEM_LIMIT),
        name="tokens",
    )(table, xbc, z, dt, *after)


def whole(array):
    return pl.BlockSpec(array.shape, lambda *_: (0,) * array.ndim)


def silu(value):
    return value / (1.0 + jnp.exp(-value))


def packet_places(groups, conv_width):
    taps_at = 2 * groups * X_WIDTH
    last_at = taps_at + 2 * groups * N
    decay_at = last_at + groups * conv_width
    return taps_at, last_at, decay_at, decay_at + LANES


def rows_kernel(plan, table, tokens, conv, weight, bias, small, gain, state, *refs):
    out, states, sems, read, read_taps, acts, wide, gates, lines = refs[-9:]
    steps = 2
    taps, groups, conv_width = weight.shape
    heads = state.shape[1]
    channels = groups * X_WIDTH
    row_ids = lax.broadcasted_iota(jnp.int32, (R_PF, 1), 0)
    live = row_ids < table[plan.live]
    f32, bf16 = jnp.float32, jnp.bfloat16
    taps_at, last_at, decay_at, _ = packet_places(groups, conv_width)

    share = heads // PARTS

    def copy(row, part):
        span = pl.ds(part * share, share)
        return pltpu.make_async_copy(
            state.at[row, span], states.at[row, span], sems.at[row * PARTS + part]
        )

    for row in range(R_PF):
        for part in range(PARTS):
            copy(row, part).start()

    matrix = one_hot(
        (R_PF, plan.places), [(row, table[plan.row_place + row]) for row in range(R_PF)]
    )
    stride = tokens.shape[2] // steps

    def rows_of(start, size):
        parts = [tokens[source, :, start : start + size] for source in range(tokens.shape[0])]
        parts = jnp.concatenate([part.astype(f32) for part in parts], axis=0)
        return pick(matrix, parts.astype(bf16))

    for group in range(groups):
        window = [
            jnp.where(live, conv[tap, group], 0.0) for tap in range(taps - 1)
        ] + [
            rows_of(step * stride + group * conv_width, conv_width) for step in range(steps)
        ]
        kernel = [weight[tap].astype(f32)[group : group + 1] for tap in range(taps)]
        offset = bias[...].astype(f32)[group : group + 1]
        parts = []
        for step in range(steps):
            total = sum(window[step + tap] * kernel[tap] for tap in range(taps)) + offset
            act = silu(total)
            acts[step, group] = act
            parts.append(act[:, X_WIDTH + N :])
        high = [part.astype(bf16).astype(f32) for part in parts]
        low = [part - near for part, near in zip(parts, high)]
        read_taps[group] = jnp.concatenate(high + low, axis=0).astype(bf16)
        start = last_at + group * conv_width
        lines[:, start : start + conv_width] = window[taps - 2]

    dts, decays = [], []
    rate = jnp.exp(small[0:1, :heads])
    for step in range(steps):
        base = step * stride + groups * conv_width
        gates[step] = silu(rows_of(base, channels))
        raw = rows_of(base + channels, LANES)[:, :heads] + small[1:2, :heads]
        dts.append(jnp.maximum(raw, 0.0) + jnp.log1p(jnp.exp(-jnp.abs(raw))))
        decays.append(jnp.exp(-dts[-1] * rate))
    lines[:, decay_at : decay_at + LANES] = jnp.concatenate(
        [jnp.where(live, decays[0] * decays[1], 0.0), jnp.zeros((R_PF, LANES - heads), f32)],
        axis=1,
    )
    skip = jnp.broadcast_to(small[2:3, :heads], (R_PF, heads))
    narrow = jnp.concatenate(dts + decays + [skip], axis=0)
    high = narrow.astype(bf16).astype(f32)
    middle = (narrow - high).astype(bf16).astype(f32)
    narrow = jnp.concatenate([high, middle, narrow - high - middle], axis=1).astype(bf16)
    head_ids = lax.broadcasted_iota(jnp.int32, (3 * heads, channels), 0) % heads
    channel_ids = lax.broadcasted_iota(jnp.int32, (3 * heads, channels), 1) // P_SIZE
    spread = pick(narrow, (head_ids == channel_ids).astype(bf16))
    for part in range(5):
        wide[part] = spread[part * R_PF : (part + 1) * R_PF]

    @pl.loop(0, R_PF)
    def _(index):
        for part in range(PARTS):
            copy(index, part).wait()
            size = share * P_SIZE
            group, start = part * size // X_WIDTH, part * size % X_WIDTH
            rows = states[index, part * share : (part + 1) * share].reshape(size, N)
            state_high, state_low = split_bf16(rows)
            dims = (((1,), (1,)), ((), ()))
            total = lax.dot_general(read_taps[group], state_high, dims, preferred_element_type=f32)
            rest = lax.dot_general(
                read_taps[group, : steps * R_PF], state_low, dims, preferred_element_type=f32
            )
            total = total[: steps * R_PF] + total[steps * R_PF :] + rest
            for step in range(steps):
                now = total[step * R_PF : (step + 1) * R_PF]
                span = slice(start, start + size)
                read[group, step, :, span] = jnp.where(
                    row_ids == index, now, read[group, step, :, span]
                )

    for group in range(groups):
        span = slice(group * X_WIDTH, (group + 1) * X_WIDTH)
        x = [acts[step, group, :, :X_WIDTH] for step in range(steps)]
        b = [acts[step, group, :, X_WIDTH : X_WIDTH + N] for step in range(steps)]
        c = [acts[step, group, :, X_WIDTH + N :] for step in range(steps)]
        u = [wide[step, :, span] * x[step] for step in range(steps)]
        first_decay, second_decay, skip = wide[2, :, span], wide[3, :, span], wide[4, :, span]
        held = [jnp.where(live, read[group, step], 0.0) for step in range(steps)]

        def pair_sum(one, two):
            return jnp.sum(one * two, axis=1, keepdims=True)

        later = second_decay * u[0]
        y = [
            first_decay * held[0] + pair_sum(b[0], c[0]) * u[0] + skip * x[0],
            second_decay * first_decay * held[1]
            + pair_sum(b[0], c[1]) * later
            + pair_sum(b[1], c[1]) * u[1]
            + skip * x[1],
        ]
        result = []
        for step in range(steps):
            gated = y[step] * gates[step, :, span]
            scale = lax.rsqrt(jnp.mean(gated * gated, axis=1, keepdims=True) + 1e-05)
            result.append(gated * scale * gain[0:1, span])
        together = jnp.concatenate(result, axis=0).astype(bf16)
        for target in range(out.shape[0]):
            out[target, :ROWS, span] = together
        lines[:, span] = later
        lines[:, channels + group * X_WIDTH : channels + (group + 1) * X_WIDTH] = u[1]
        for step in range(steps):
            start = taps_at + (step * groups + group) * N
            lines[:, start : start + N] = b[step]
    segments = lines.shape[1] // channels
    values = [lines[:, part * channels : (part + 1) * channels] for part in range(segments)]
    high = [value.astype(bf16).astype(f32) for value in values]
    low = [value - near for value, near in zip(values, high)]
    pairs = []
    for row in range(R_PF):
        place = table[plan.row_place + row]
        first = place // plan.cap * ROWS + place % plan.cap * 2 * segments
        pairs += [(first + part, part * R_PF + row) for part in range(2 * segments)]
    matrix = one_hot((out.shape[0] * ROWS, 2 * segments * R_PF), pairs)
    placed = pick(matrix, jnp.concatenate(high + low, axis=0).astype(bf16)).astype(bf16)
    for target in range(out.shape[0]):
        out[target, ROWS:] = placed[target * ROWS : (target + 1) * ROWS]


def run_rows(plan, table, tokens, conv, weight, bias, small, gain, ssm_state, after):
    taps, groups, conv_width = weight.shape
    steps = 2
    heads = ssm_state.shape[1]
    sources = plan.places // plan.cap
    channels = groups * X_WIDTH
    size = -(-packet_places(groups, conv_width)[-1] // channels) * channels
    f32 = jnp.float32
    return pl.pallas_call(
        functools.partial(rows_kernel, plan),
        grid_spec=pltpu.PrefetchScalarGridSpec(
            num_scalar_prefetch=1,
            grid=(1,),
            in_specs=[
                whole(tokens),
                whole(conv),
                whole(weight),
                whole(bias),
                whole(small),
                whole(gain),
                HBM,
            ]
            + [ANY] * len(after),
            out_specs=pl.BlockSpec((sources, 2 * ROWS, channels), lambda i, t: (0, 0, 0)),
            scratch_shapes=[
                pltpu.VMEM((R_PF, heads, P_SIZE, N), f32),
                pltpu.SemaphoreType.DMA((R_PF * PARTS,)),
                pltpu.VMEM((groups, steps, R_PF, X_WIDTH), f32),
                pltpu.VMEM((groups, 2 * steps * R_PF, N), jnp.bfloat16),
                pltpu.VMEM((steps, groups, R_PF, conv_width), f32),
                pltpu.VMEM((5, R_PF, channels), f32),
                pltpu.VMEM((steps, R_PF, channels), f32),
                pltpu.VMEM((R_PF, size), f32),
            ],
        ),
        out_shape=jax.ShapeDtypeStruct((sources, 2 * ROWS, channels), jnp.bfloat16),
        compiler_params=pltpu.CompilerParams(vmem_limit_bytes=VMEM_LARGE),
        name="rows",
    )(table, tokens, conv, weight, bias, small, gain, ssm_state, *after)


def project_kernel(plan, share, table, normed, weight, *refs):
    steps = 2
    targets = plan.rows // share
    own, out, held, total, picked, sems = refs[-6:]
    depth = weight.shape[0]
    piece = depth // BLOCKS

    def copy(block):
        span = pl.ds(block * piece, piece)
        return pltpu.make_async_copy(weight.at[span], held.at[span], sems.at[block])

    for block in range(BLOCKS):
        copy(block).start()

    shape = (steps * plan.rows, steps * plan.rows)
    rows = lax.broadcasted_iota(jnp.int32, shape, 0)
    columns = lax.broadcasted_iota(jnp.int32, shape, 1)

    def add(slot, matrix):
        row = table[plan.slot_row + slot]
        target = slot // share * steps * share + slot % share
        source = (row // R_PF) * steps * R_PF + row % R_PF
        for step in range(steps):
            hit = (rows == target + step * share) & (columns == source + step * R_PF)
            matrix = jnp.where(hit, 1.0, matrix)
        return matrix

    matrix = lax.fori_loop(0, plan.rows, add, jnp.zeros(shape, jnp.float32), unroll=8)
    values = normed[...].reshape(picked.shape)
    picked[...] = pick(matrix.astype(jnp.bfloat16), values).astype(jnp.bfloat16)
    for block in range(BLOCKS):
        copy(block).wait()
        span = slice(block * piece, (block + 1) * piece)
        part = pick(picked[:, span], held[span])
        total[...] = part if block == 0 else total[...] + part
    for target in range(targets):
        part = total[target * steps * share : (target + 1) * steps * share]
        out[target] = part.astype(out.dtype)

        @pl.when(table[plan.head] == target)
        def _():
            own[...] = part


def project(plan, share, table, normed, weight, after):
    depth, columns = weight.shape
    rows = 2 * share
    targets = plan.rows // share
    own = jax.ShapeDtypeStruct((rows, columns), jnp.float32)
    out = jax.ShapeDtypeStruct((targets, rows, columns), jnp.bfloat16)
    return pl.pallas_call(
        functools.partial(project_kernel, plan, share),
        grid_spec=pltpu.PrefetchScalarGridSpec(
            num_scalar_prefetch=1,
            grid=(1,),
            in_specs=[pl.BlockSpec((normed.shape[0], ROWS, depth), lambda i, t: (0, 0, 0)), HBM]
            + [ANY] * len(after),
            out_specs=[whole(own), whole(out)],
            scratch_shapes=[
                pltpu.VMEM(weight.shape, jnp.bfloat16),
                pltpu.VMEM((2 * plan.rows, columns), jnp.float32),
                pltpu.VMEM((2 * plan.rows, depth), jnp.bfloat16),
                pltpu.SemaphoreType.DMA((BLOCKS,)),
            ],
        ),
        out_shape=[own, out],
        compiler_params=pltpu.CompilerParams(vmem_limit_bytes=VMEM_LARGE),
        name="project",
    )(table, normed, weight, *after)


def slots_kernel(plan, decay_at, table, packets, xbc, *refs):
    own, other = refs[-2:]
    f32, bf16 = jnp.float32, jnp.bfloat16
    steps, groups = xbc.shape[:2]
    half = R_PF // 2
    sources, _, channels = packets.shape
    segments = (own.shape[1] - LANES - steps * groups * xbc.shape[3]) // channels
    pairs, order = [], []
    for local in range(R_PF):
        slot = (local + table[plan.parity] * half) % R_PF
        order.append((local, slot))
        place = table[plan.slot_place + slot]
        first = place // plan.cap * ROWS + place % plan.cap * 2 * segments
        pairs += [(part * R_PF + local, first + part) for part in range(2 * segments)]
    matrix = one_hot((2 * segments * R_PF, sources * ROWS), pairs)
    order = one_hot((R_PF, R_PF), order)

    def put(values, start):
        size = values.shape[1]
        own[:, start : start + size] = values[:half].astype(bf16)
        other[:, start : start + size] = values[half:].astype(bf16)

    picked = pick(matrix, packets[...].reshape(sources * ROWS, channels))
    for part in range(segments):
        high = picked[part * R_PF : (part + 1) * R_PF]
        low = picked[(segments + part) * R_PF : (segments + part + 1) * R_PF]
        put(high + low, part * channels)
        if decay_at // channels == part:
            span = slice(decay_at % channels, decay_at % channels + LANES)
            put(low[:, span], segments * channels)
    at = segments * channels + LANES
    for step in range(steps):
        for group in range(groups):
            put(pick(order, xbc[step, group]), at)
            at += xbc.shape[3]


def split_slots(plan, table, packets, xbc, after):
    steps, groups, _, conv_width = xbc.shape
    sources, _, channels = packets.shape
    decay_at, end = packet_places(groups, conv_width)[2:]
    size = -(-end // channels) * channels + LANES + steps * groups * conv_width
    out = jax.ShapeDtypeStruct((R_PF // 2, size), jnp.bfloat16)
    return pl.pallas_call(
        functools.partial(slots_kernel, plan, decay_at),
        grid_spec=pltpu.PrefetchScalarGridSpec(
            num_scalar_prefetch=1,
            grid=(1,),
            in_specs=[
                pl.BlockSpec((sources, ROWS, channels), lambda i, t: (0, 1, 0)),
                whole(xbc),
            ]
            + [ANY] * len(after),
            out_specs=[whole(out)] * 2,
        ),
        out_shape=[out, out],
        compiler_params=pltpu.CompilerParams(vmem_limit_bytes=VMEM_LIMIT),
        name="slots",
    )(table, packets, xbc, *after)


def windows_kernel(plan, groups, conv_width, starts, table, own, got, *refs):
    out = refs[-1]
    parity = table[plan.parity]
    for owner, packet in enumerate((own, got)):
        side = jnp.where(parity == owner, 0, groups)
        for row, start in enumerate(starts):
            for group in range(groups):
                first = start + group * conv_width
                values = packet[:, first : first + conv_width].astype(jnp.float32)
                for slot in range(R_PF // 2):
                    out[0, 0, slot, row, pl.ds(side + group, 1)] = values[slot : slot + 1]


def write_windows(plan, table, own, got, groups, conv_width, starts, after):
    shape = (1, 1, R_PF // 2, len(starts), 2 * groups, conv_width)
    out = jax.ShapeDtypeStruct(shape, jnp.float32)
    return pl.pallas_call(
        functools.partial(windows_kernel, plan, groups, conv_width, starts),
        grid_spec=pltpu.PrefetchScalarGridSpec(
            num_scalar_prefetch=1,
            grid=(1,),
            in_specs=[whole(own), whole(got)] + [ANY] * len(after),
            out_specs=whole(out),
        ),
        out_shape=out,
        compiler_params=pltpu.CompilerParams(vmem_limit_bytes=VMEM_LIMIT),
        name="windows",
    )(table, own, got, *after)


def pack_kernel(plan, places, first, table, state, *refs):
    rows, sems = refs[-2:]
    outputs = refs[-2 - len(places) // plan.cap : -2]
    width = rows.shape[1]

    def copy(index):
        row = table[plan.row_of + places[index]]
        return pltpu.make_async_copy(
            state.at[row, pl.ds(first, width)], rows.at[index], sems.at[index]
        )

    for index in range(len(places)):
        copy(index).start()
    for index in range(len(places)):
        copy(index).wait()
        outputs[index // plan.cap][index % plan.cap] = rows[index].astype(jnp.bfloat16)


def pack_rows(plan, table, ssm_state, shifts, first, width, after):
    cap = plan.cap
    places = [shift * cap + rank for shift in shifts for rank in range(cap)]
    out = jax.ShapeDtypeStruct((cap, width, P_SIZE, N), jnp.bfloat16)
    return pl.pallas_call(
        functools.partial(pack_kernel, plan, places, first),
        grid_spec=pltpu.PrefetchScalarGridSpec(
            num_scalar_prefetch=1,
            grid=(1,),
            in_specs=[HBM] + [ANY] * len(after),
            out_specs=[whole(out)] * len(shifts),
            scratch_shapes=[
                pltpu.VMEM((len(places), width, P_SIZE, N), jnp.float32),
                pltpu.SemaphoreType.DMA((len(places),)),
            ],
        ),
        out_shape=[out] * len(shifts),
        compiler_params=pltpu.CompilerParams(vmem_limit_bytes=VMEM_LIMIT),
        name=f"pack_{first}_{width}",
    )(table, ssm_state, *after)


def route_kernel(plan, sources, nears, offset, table, *refs):
    cap = plan.cap
    arrived, keep, give = refs[:sources], refs[-2], refs[-1]
    half = keep.shape[0]
    for index in range(2 * half):
        target = keep if index < half else give
        place = table[plan.split_place + index]
        for source in range(sources):

            @pl.when(place // cap == source)
            def _():
                if source < nears:
                    span = pl.ds(offset, target.shape[1])
                    target[index % half] = arrived[source][place % cap, span]
                else:
                    target[index % half] = arrived[source][place % cap]


def route_chunk(plan, table, near, far, first, offset, after):
    width = far[0].shape[1]
    half = R_PF // 2
    out = jax.ShapeDtypeStruct((half, width, P_SIZE, N), jnp.bfloat16)
    return pl.pallas_call(
        functools.partial(route_kernel, plan, len(near) + len(far), len(near), offset),
        grid_spec=pltpu.PrefetchScalarGridSpec(
            num_scalar_prefetch=1,
            grid=(1,),
            in_specs=[whole(one) for one in [*near, *far]] + [ANY] * len(after),
            out_specs=[whole(out)] * 2,
        ),
        out_shape=[out, out],
        compiler_params=pltpu.CompilerParams(vmem_limit_bytes=VMEM_LIMIT),
        name=f"route_{first}_{width}",
    )(table, *near, *far, *after)


def finish_kernel(plan, width, heads, base, table, decay, keep, got, *refs):
    parts, out, done = refs[:8], refs[-2], refs[-1]
    owner = pl.program_id(0)
    slots = keep.shape[0]
    done[...] = jnp.zeros_like(done)

    def fill(source, *pieces):
        first_update, second_update, first_taps, second_taps = [
            piece[...].astype(jnp.float32) for piece in pieces
        ]

        def stack(first, second, slot):
            blank = jnp.zeros((6, first.shape[1]), jnp.float32)
            rows = [first[slot : slot + 1], second[slot : slot + 1], blank]
            return jnp.concatenate(rows, axis=0).astype(jnp.bfloat16)

        for slot in range(slots):
            added = lax.dot_general(
                stack(first_update, second_update, slot),
                stack(first_taps, second_taps, slot),
                (((0,), (0,)), ((), ())),
                preferred_element_type=jnp.float32,
            ).reshape(width, P_SIZE, N)
            for head in range(width):
                factor = decay[(owner * slots + slot) * heads + base + head]
                out[0, 0, slot, head] = (
                    factor * source[slot, head].astype(jnp.float32) + added[head]
                )

    pl.when(owner == 0)(lambda: fill(keep, *parts[:4]))
    pl.when(owner == 1)(lambda: fill(got, *parts[4:]))


def finish_chunk(plan, table, so_far, keep, got, decay, own, other, first, heads):
    slots, width = keep.shape[:2]
    per_half = heads // width
    span = width * P_SIZE
    channels = heads * P_SIZE
    groups = heads // PER_GROUP
    group = first // PER_GROUP
    chunk = first // width
    taps_at = 2 * channels // N
    out_shape = jax.ShapeDtypeStruct((1, 1, slots, 2 * heads, P_SIZE, N), jnp.float32)
    extra = [so_far]

    def part(size, place):
        return pl.BlockSpec((slots, size), lambda o, t, d: (0, place))

    parts = [
        part(span, chunk),
        part(span, channels // span + chunk),
        part(N, taps_at + group),
        part(N, taps_at + groups + group),
    ]
    side = lambda o, t: (o + t[plan.parity]) % 2
    return pl.pallas_call(
        functools.partial(finish_kernel, plan, width, heads, first),
        grid_spec=pltpu.PrefetchScalarGridSpec(
            num_scalar_prefetch=2,
            grid=(2,),
            in_specs=[whole(keep), whole(got)] + parts + parts + [ANY] * len(extra),
            out_specs=[
                pl.BlockSpec(
                    (1, 1, slots, width, P_SIZE, N),
                    lambda o, t, d: (0, 0, 0, side(o, t) * per_half + chunk, 0, 0),
                ),
                pl.BlockSpec((8, 128), lambda o, t, d: (0, 0)),
            ],
        ),
        out_shape=[out_shape, jax.ShapeDtypeStruct((8, 128), jnp.float32)],
        input_output_aliases={12: 0} if so_far.shape == out_shape.shape else {},
        compiler_params=pltpu.CompilerParams(vmem_limit_bytes=VMEM_LIMIT),
        name=f"finish_{first}_{width}",
    )(table, decay, keep, got, *([own] * 4), *([other] * 4), *extra)


def on_device(
    ssm_state,
    conv_state,
    counts,
    request_slot,
    token_xbc,
    token_z,
    token_dt,
    conv_weight,
    conv_bias,
    a_log,
    dt_bias,
    d_skip,
    norm_gain,
    out_weight,
):
    f32 = jnp.float32
    req_count = lax.axis_size("req")
    head_count = lax.axis_size("head")
    plan = Plan(req_count)
    steps = token_xbc.shape[0]
    heads = ssm_state.shape[1]
    groups = conv_state.shape[2]
    conv_width = conv_state.shape[3]
    channels = groups * X_WIDTH

    def shifted(value, axis, shift):
        return lax.ppermute(value, axis, [(i, i ^ shift) for i in range(lax.axis_size(axis))])

    def swap(value):
        return shifted(value, "head", 1)

    def exchange(value, axis):
        return lax.all_to_all(value, axis, split_axis=0, concat_axis=0, tiled=True)

    table = make_plan(plan, request_slot, counts)

    unit = heads // UNITS
    count = len(CHUNKS)
    firsts = [start * unit for start, _ in CHUNKS]
    far, sent = [None] * count, [None] * count
    keeps, gives, gots = [None] * count, [None] * count, [None] * count

    def send(chunk, shifts, after):
        width = CHUNKS[chunk][1] * unit
        packed = pack_rows(plan, table, ssm_state, shifts, firsts[chunk], width, after)
        sent[chunk] = packed[0]
        return [shifted(part, "req", shift) if shift else part for part, shift in zip(packed, shifts)]

    def route(chunk, near, far, after):
        keeps[chunk], gives[chunk] = route_chunk(
            plan, table, near, far, firsts[chunk], firsts[chunk] - CHUNKS[0][1] * unit, after
        )
        gots[chunk] = swap(gives[chunk])

    xbc = jnp.swapaxes(token_xbc, 1, 2)
    all_shifts, far_shifts = range(req_count), range(NEAR, req_count)
    far[0] = send(0, all_shifts, [])
    packed_tokens = pack_tokens(plan, table, xbc, token_z, token_dt, [sent[0]])
    tokens = exchange(packed_tokens, "req")
    far[1] = send(1, far_shifts, [packed_tokens])
    route(0, [], far[0], [sent[1], tokens])
    rest = UNITS - CHUNKS[0][1]
    near = pack_rows(
        plan, table, ssm_state, range(NEAR), CHUNKS[0][1] * unit, rest * unit, [sent[1]]
    )
    far[2] = send(2, far_shifts, [gives[0]])
    near = [near[0]] + [shifted(near[shift], "req", shift) for shift in range(1, NEAR)]

    small = jnp.stack([a_log, dt_bias, d_skip]).astype(f32)
    result = run_rows(
        plan,
        table,
        tokens,
        jnp.moveaxis(conv_state, 0, 2),
        conv_weight,
        conv_bias,
        small,
        norm_gain.astype(f32)[None],
        ssm_state,
        [gives[0]],
    )
    route(1, near, far[1], [sent[2], gots[0], result])
    result = exchange(result, "req")
    share = plan.rows // head_count
    own_sum, sums = project(plan, share, table, result, out_weight, [gives[1]])
    others = exchange(sums, "head").astype(f32)
    is_mine = jnp.arange(head_count) == lax.axis_index("head")
    layer_out = own_sum + jnp.sum(jnp.where(is_mine[:, None, None], 0.0, others), axis=0)
    layer_out = layer_out.astype(jnp.bfloat16).reshape(steps, share, -1)

    own, give = split_slots(plan, table, result, xbc, far[2])
    other = swap(give)
    route(2, near, far[2], [other, gots[1]])
    _, last_at, decay_at, end = packet_places(groups, conv_width)
    low_at = -(-end // channels) * channels
    fresh_at = low_at + LANES
    starts = [last_at] + [fresh_at + step * groups * conv_width for step in range(steps)]
    both = jnp.stack([own, other]).astype(f32)
    decay = both[:, :, decay_at : decay_at + heads] + both[:, :, low_at : low_at + heads]
    decay = decay.reshape(-1)
    out_conv = write_windows(
        plan, table, own, other, groups, conv_width, starts, [gives[2]]
    )

    out_ssm = gives[-1]
    for chunk in range(count):
        out_ssm, done = finish_chunk(
            plan, table, out_ssm, keeps[chunk], gots[chunk], decay, own, other, firsts[chunk], heads
        )
    return (layer_out, out_ssm, out_conv)


def solution(mesh):
    in_specs = (
        P(("groups", "req"), "head", None, None),
        P(("groups", "req"), None, "head", None),
        P("groups"),
        P("groups"),
        P(None, ("groups", "req"), "head", None),
        P(None, ("groups", "req"), "head"),
        P(None, ("groups", "req"), "head"),
        P(None, "head", None),
        P("head", None),
        P("head"),
        P("head"),
        P("head"),
        P("head"),
        P("head", "req"),
    )
    out_specs = (
        P(None, ("groups", "head"), "req"),
        P(("groups", "req"), "head", None, None, None, None),
        P(("groups", "req"), "head", None, None, None, None),
    )
    return jax.shard_map(
        on_device, mesh=mesh, in_specs=in_specs, out_specs=out_specs, check_vma=False
    )
```
